128 devices in a mesh: row: 8 (over y_lo, x), col: 16 (over z, y_hi, core).
Axes of the slice: x: 4, y: 4 (y_hi: 2, y_lo: 2; y = y_hi * 2 + y_lo), z: 4, core: 2. Of those that a mesh axis runs over, the one named last changes fastest.
Arguments:
- design: float32 [16384, 16384], P('row', 'col'), may hold values from -1 to 1
- coefficients: float32 [2, 8], replicated, may hold values from -3 to 3
- focal_steps: int32 [2], replicated, may hold values from 1 to 63, as said below
- target: float32 [2, 128, 128], replicated, may hold values from 0 to 2
Outputs:
- gradient: float32 [16384, 16384], P('row', 'col')
- field: float32 [2, 2, 128, 128], replicated
The draws below stay inside these ranges and needn't reach their ends.
Inputs may be any that keep to these rules, and one draw needn't show every extreme that they name: `focal_steps`: every chirp rate is odd, and one of them is 63.
All inputs are finite; a program needn't handle non-finite values.
Results may differ from the reference program's by a relative error of at most 0.0073.
Values sent between devices are 32-bit elements; how exact they have to be, the bound alone decides.
A program may use at most 128 MiB of HBM per device.

```python
import math
import jax
import jax.numpy as jnp
from jax import lax

FOCAL = 128
DEPTHS = 2
TERMS = 8
NR = 16384
NC = 16384


def draw_focal_steps(key, part):
    key = jax.random.fold_in(key, 5)
    rate_key, place_key = jax.random.split(key)
    rates = 2 * jax.random.randint(rate_key, (DEPTHS,), 0, 32, dtype=jnp.int32) + 1
    chosen = jax.random.randint(place_key, (), 0, DEPTHS, dtype=jnp.int32)
    return jnp.where(jnp.arange(DEPTHS, dtype=jnp.int32) == chosen, jnp.int32(63), rates)


def block_levels(own_key, shape, shards, low, largest):
    level = 1.0
    for dim, shards_of in shards:
        steps = jax.random.uniform(jax.random.fold_in(jax.random.fold_in(own_key, 6), dim), (shards_of,), jnp.float32, low / len(shards), largest / len(shards))
        level = level * jnp.repeat(jnp.exp(steps), shape[dim] // shards_of).reshape((-1,) + (1,) * (len(shape) - 1 - dim))
    return level


def noise(own_key, extent, scale, limit, held_as=jnp.bfloat16):
    return jnp.clip(scale * jax.random.normal(own_key, extent, jnp.float32), -limit, limit).astype(held_as)


def setup_inputs(seed: int = 0) -> dict:
    streams_of = jax.random.split(jax.random.key(seed), 5)
    return {
        "design": jnp.clip(jax.random.uniform(streams_of[0], (NR, NC), jnp.float32, -1.0, 1.0) * block_levels(streams_of[0], (NR, NC), ((0, 8), (1, 16)), -0.4, 0.0), -1.0, 1.0),
        "coefficients": noise(streams_of[1], (2, TERMS), 0.5, 3.0, jnp.float32),
        "focal_steps": draw_focal_steps(jax.random.fold_in(streams_of[4], 71), 0),
        "target": jnp.clip(jax.random.uniform(streams_of[3], (DEPTHS, FOCAL, FOCAL), jnp.float32, 0.0, 2.0), 0.0, 2.0),
    }


def chirp_pair(positions, total, step):
    window = jnp.arange(FOCAL, dtype=jnp.int32) + (total // 2 - FOCAL // 2)
    period = 2 * total
    offset = jnp.mod(window[:, None] - positions[None, :], period)
    phase_index = jnp.mod(jnp.mod(offset * offset, period) * step, period)
    angle = jnp.pi * phase_index.astype(jnp.float32) / total
    scale = 1.0 / math.sqrt(total)
    return ((jnp.cos(angle) * scale).astype(jnp.bfloat16), (jnp.sin(angle) * scale).astype(jnp.bfloat16))

def transmission(design, coefficients):
    t_prev = jnp.ones_like(design)
    t_cur = design
    u_prev = jnp.ones_like(design)
    u_cur = 2.0 * design
    real_part = coefficients[0, 0] + coefficients[0, 1] * design
    imag_part = coefficients[1, 0] + coefficients[1, 1] * design
    real_slope = coefficients[0, 1] * t_prev
    imag_slope = coefficients[1, 1] * t_prev
    for order in range(2, TERMS):
        t_next = 2.0 * design * t_cur - t_prev
        real_part = real_part + coefficients[0, order] * t_next
        imag_part = imag_part + coefficients[1, order] * t_next
        real_slope = real_slope + coefficients[0, order] * order * u_cur
        imag_slope = imag_slope + coefficients[1, order] * order * u_cur
        t_prev, t_cur = (t_cur, t_next)
        u_prev, u_cur = (u_cur, 2.0 * design * u_cur - u_prev)
    return (real_part, imag_part, real_slope, imag_slope)

def exact(left, right):
    return jnp.dot(left, right, precision=lax.Precision.HIGHEST, preferred_element_type=jnp.float32)

def reference(design, coefficients, focal_steps, target):
    block = min(NR, 1024)
    blocks = NR // block
    col_tables = [chirp_pair(jnp.arange(NC, dtype=jnp.int32), NC, focal_steps[depth]) for depth in range(DEPTHS)]

    def forward_block(carry, index):
        rows = lax.dynamic_slice_in_dim(design, index * block, block, 0)
        real_part, imag_part, unused_a, unused_b = transmission(rows, coefficients)
        real_b = real_part.astype(jnp.bfloat16)
        imag_b = imag_part.astype(jnp.bfloat16)
        positions = index * block + jnp.arange(block, dtype=jnp.int32)
        fields = []
        for depth in range(DEPTHS):
            row_r, row_i = chirp_pair(positions, NR, focal_steps[depth])
            col_r, col_i = col_tables[depth]
            part_r = jnp.dot(real_b, col_r.T, preferred_element_type=jnp.float32) - jnp.dot(imag_b, col_i.T, preferred_element_type=jnp.float32)
            part_i = jnp.dot(real_b, col_i.T, preferred_element_type=jnp.float32) + jnp.dot(imag_b, col_r.T, preferred_element_type=jnp.float32)
            row_r32 = row_r.astype(jnp.float32)
            row_i32 = row_i.astype(jnp.float32)
            field_r = exact(row_r32, part_r) - exact(row_i32, part_i)
            field_i = exact(row_r32, part_i) + exact(row_i32, part_r)
            fields.append(jnp.stack([field_r, field_i]))
        return (carry + jnp.stack(fields), None)
    start = jnp.zeros((DEPTHS, 2, FOCAL, FOCAL), jnp.float32)
    field, unused = lax.scan(forward_block, start, jnp.arange(blocks, dtype=jnp.int32))
    factor = math.sqrt(NR * NC) / (4.0 * FOCAL)
    excess = field[:, 0] * field[:, 0] + field[:, 1] * field[:, 1] - target
    grad_r = 4.0 * factor * excess * field[:, 0]
    grad_i = 4.0 * factor * excess * field[:, 1]

    def backward_block(index):
        rows = lax.dynamic_slice_in_dim(design, index * block, block, 0)
        real_part, imag_part, real_slope, imag_slope = transmission(rows, coefficients)
        positions = index * block + jnp.arange(block, dtype=jnp.int32)
        sum_r = jnp.zeros((block, NC), jnp.float32)
        sum_i = jnp.zeros((block, NC), jnp.float32)
        for depth in range(DEPTHS):
            row_r, row_i = chirp_pair(positions, NR, focal_steps[depth])
            col_r, col_i = col_tables[depth]
            row_r32 = row_r.astype(jnp.float32).T
            row_i32 = row_i.astype(jnp.float32).T
            back_r = (exact(row_r32, grad_r[depth]) + exact(row_i32, grad_i[depth])).astype(jnp.bfloat16)
            back_i = (exact(row_i32, grad_r[depth]) - exact(row_r32, grad_i[depth])).astype(jnp.bfloat16)
            sum_r = sum_r + jnp.dot(back_r, col_r, preferred_element_type=jnp.float32) - jnp.dot(back_i, col_i, preferred_element_type=jnp.float32)
            sum_i = sum_i + jnp.dot(back_r, col_i, preferred_element_type=jnp.float32) + jnp.dot(back_i, col_r, preferred_element_type=jnp.float32)
        return real_slope * sum_r - imag_slope * sum_i
    gradient = lax.map(backward_block, jnp.arange(blocks, dtype=jnp.int32)).reshape(NR, NC)
    return (gradient, field)
```

```python
import functools
import math

import jax
import jax.numpy as jnp
from jax import lax
from jax.experimental import pallas as pl
from jax.experimental.pallas import tpu as pltpu
from jax.sharding import PartitionSpec as P

MESH = pl.DeviceIdType.MESH
F32, BF16 = jnp.float32, jnp.bfloat16
AXIS = 4
CHIPS = 64
CHUNK = 256


def hops(off):
    return sum(min(a, AXIS - a) for a in off)


OFFSETS = sorted(
    (
        (a, b, c)
        for a in range(AXIS)
        for b in range(AXIS)
        for c in range(AXIS)
        if (a, b, c) != (0, 0, 0)
    ),
    key=lambda off: -hops(off),
)


def coords():
    row, col = lax.axis_index("row"), lax.axis_index("col")
    x, y_lo = row % 4, row // 4
    core, y_hi, z = col % 2, (col // 2) % 2, col // 4
    return x, y_hi * 2 + y_lo, z, core


def device(x, y, z, core):
    return ((y % 2) * 4 + x, (z * 2 + y // 2) * 2 + core)


def monomials(c):
    return [
        c[0] - c[2] + c[4] - c[6],
        c[1] - 3.0 * c[3] + 5.0 * c[5] - 7.0 * c[7],
        2.0 * c[2] - 8.0 * c[4] + 18.0 * c[6],
        4.0 * c[3] - 20.0 * c[5] + 56.0 * c[7],
        8.0 * c[4] - 48.0 * c[6],
        16.0 * c[5] - 112.0 * c[7],
        32.0 * c[6],
        64.0 * c[7],
    ]


def horner(x, coefs):
    acc = coefs[-1] * x + coefs[-2]
    for c in coefs[-3::-1]:
        acc = acc * x + c
    return acc


def chirp_rows(first, width, total, steps):
    shape = (8, width)
    u = lax.broadcasted_iota(jnp.int32, shape, 1) + first
    r = lax.broadcasted_iota(jnp.int32, shape, 0)
    mask = 2 * total - 1
    step = jnp.where((r & 2) == 0, steps[0], steps[1])
    off = u & mask
    k = (((off * off) & mask) * step) & mask
    k = (k - (r & 1) * (total // 2)) & mask
    p = total // 2 - jnp.minimum(k, 2 * total - k)
    a = p.astype(F32) * (math.pi / total)
    s = a * a
    poly = horner(s, [(-1.0) ** n / math.factorial(2 * n + 1) for n in range(7)])
    return a * poly * (1.0 / math.sqrt(total))


def across(seq, r, width):
    x = jnp.broadcast_to(seq[r : r + 1, :], (128, width + 128))
    return pltpu.roll(x, 0, 1, stride=1, stride_axis=0)[:, 128:]


def down(seq, r, block, blocks):
    lo = (blocks - 1 - block) * 128
    x = jnp.broadcast_to(seq[r : r + 1, lo : lo + 256], (128, 256))
    return pltpu.roll(x, 0, 1, stride=1, stride_axis=0)[:, 128:]


def forward_kernel(
    total,
    design_hbm,
    coef,
    steps,
    field_ref,
    dtr_ref,
    dti_ref,
    at_ref,
    wb_ref,
    x_ref,
    t0,
    t1,
    wcol,
    rtab,
    qh,
    ql,
    partial,
    sib,
    pieces,
    landed,
    load_sem,
    sib_send,
    sib_recv,
    rs_send,
    rs_recv,
    ag_send,
    ag_recv,
):
    rows, cols = x_ref.shape
    chunks = rows // CHUNK
    x, y, z, core = coords()
    chip = (x * AXIS + y) * AXIS + z
    other = 1 - core
    sibling = device(x, y, z, other)

    def peer(off):
        px, py, pz = (x + off[0]) % AXIS, (y + off[1]) % AXIS, (z + off[2]) % AXIS
        return (px * AXIS + py) * AXIS + pz, device(px, py, pz, core)

    loads = []
    for i in range(chunks):
        part = pl.ds(i * CHUNK, CHUNK)
        load = pltpu.make_async_copy(design_hbm.at[part], x_ref.at[part], load_sem.at[i])
        load.start()
        loads.append(load)

    barrier = pltpu.get_barrier_semaphore()
    pl.semaphore_signal(barrier, inc=1, device_id=sibling, device_id_type=MESH)
    for off in OFFSETS:
        pl.semaphore_signal(barrier, inc=1, device_id=peer(off)[1], device_id_type=MESH)

    step = [steps[0], steps[1]]
    first_row = lax.axis_index("row") * rows - (total // 2 - 64)
    first_col = lax.axis_index("col") * cols - (total // 2 - 64)
    mono = [monomials([coef[i, k] for k in range(8)]) for i in range(2)]

    seq = chirp_rows(-first_col - cols, cols + 128, total, step)
    for d in range(2):
        for b in range(cols // 128):
            re = down(seq, 2 * d, b, cols // 128).astype(BF16)
            im = down(seq, 2 * d + 1, b, cols // 128).astype(BF16)
            j = b * 128
            wcol[j : j + 128, 256 * d : 256 * d + 128] = re
            wcol[j : j + 128, 256 * d + 128 : 256 * d + 256] = im
            wcol[cols + j : cols + j + 128, 256 * d : 256 * d + 128] = -im
            wcol[cols + j : cols + j + 128, 256 * d + 128 : 256 * d + 256] = re
    seq = chirp_rows(first_row - 128, rows + 128, total, step)
    for r in range(4):
        rtab[128 * r : 128 * r + 128, :] = across(seq, r, rows).astype(BF16)

    def transmit(i, t):
        loads[i].wait()
        v = x_ref[i * CHUNK : (i + 1) * CHUNK, :]
        t[:, :cols] = horner(v, mono[0]).astype(BF16)
        t[:, cols:] = horner(v, mono[1]).astype(BF16)

    def contract(i, t):
        q = jnp.dot(t[...], wcol[...], preferred_element_type=F32)
        hi = q.astype(BF16)
        qh[i * CHUNK : (i + 1) * CHUNK, :] = hi
        ql[i * CHUNK : (i + 1) * CHUNK, :] = (q - hi.astype(F32)).astype(BF16)

    slots = [t0, t1]
    transmit(0, t0)
    for i in range(chunks):
        if i + 1 < chunks:
            transmit(i + 1, slots[(i + 1) % 2])
        contract(i, slots[i % 2])

    def focus(d):
        a = rtab[pl.ds(d * 256, 256), :]
        lanes = pl.ds(d * 256, 256)
        f = jnp.dot(a, qh[:, lanes], preferred_element_type=F32) + jnp.dot(
            a, ql[:, lanes], preferred_element_type=F32
        )
        return jnp.concatenate(
            [f[:128, :128] - f[128:, 128:], f[:128, 128:] + f[128:, :128]], axis=0
        )

    partial[...] = focus(other)
    pl.semaphore_wait(barrier, CHIPS)
    give = pltpu.make_async_remote_copy(
        src_ref=partial,
        dst_ref=sib,
        send_sem=sib_send.at[0],
        recv_sem=sib_recv.at[0],
        device_id=sibling,
        device_id_type=MESH,
    )
    give.start()
    own = focus(core)
    give.wait_recv()
    total_chip = own + sib[...]
    for p in range(CHIPS):
        pieces[p] = total_chip[4 * p : 4 * p + 4, :]

    sends = []
    for n, off in enumerate(OFFSETS):
        there, dev = peer(off)
        copy = pltpu.make_async_remote_copy(
            src_ref=pieces.at[there],
            dst_ref=landed.at[n],
            send_sem=rs_send,
            recv_sem=rs_recv,
            device_id=dev,
            device_id_type=MESH,
        )
        copy.start()
        sends.append(copy)

    slopes = [[k * m[k] for k in range(1, 8)] for m in mono]

    @pl.loop(0, rows // 64)
    def _(i):
        part = pl.ds(pl.multiple_of(i * 64, 64), 64)
        v = x_ref[part]
        dtr_ref[part] = horner(v, slopes[0])
        dti_ref[part] = horner(v, slopes[1])

    everything = pl.ds(0, CHIPS - 1)
    pltpu.make_async_copy(landed.at[everything], landed.at[everything], rs_recv).wait()
    total_piece = pieces[chip]
    for n in range(CHIPS - 1):
        total_piece = total_piece + landed[n]
    mine = field_ref.at[core]
    mine[chip] = total_piece
    for n, off in enumerate(OFFSETS):
        dev = peer(off)[1]
        copy = pltpu.make_async_remote_copy(
            src_ref=mine.at[chip],
            dst_ref=mine.at[chip],
            send_sem=ag_send,
            recv_sem=ag_recv,
            device_id=dev,
            device_id_type=MESH,
        )
        copy.start()

    seq = chirp_rows(-first_row - rows, rows + 128, total, step)
    for r in range(4):
        for b in range(rows // 128):
            at_ref[128 * b : 128 * b + 128, 128 * r : 128 * r + 128] = down(
                seq, r, b, rows // 128
            ).astype(BF16)
    seq = chirp_rows(first_col - 128, cols + 128, total, step)
    for d in range(2):
        re = across(seq, 2 * d, cols).astype(BF16)
        im = across(seq, 2 * d + 1, cols).astype(BF16)
        wb_ref[256 * d : 256 * d + 128, :cols] = re
        wb_ref[256 * d : 256 * d + 128, cols:] = im
        wb_ref[256 * d + 128 : 256 * d + 256, :cols] = -im
        wb_ref[256 * d + 128 : 256 * d + 256, cols:] = re

    pltpu.make_async_copy(mine.at[everything], mine.at[everything], ag_recv).wait()
    show = pltpu.make_async_remote_copy(
        src_ref=mine,
        dst_ref=field_ref.at[core],
        send_sem=sib_send.at[1],
        recv_sem=sib_recv.at[1],
        device_id=sibling,
        device_id_type=MESH,
    )
    show.start()
    show.wait_recv()
    give.wait_send()
    pltpu.make_async_copy(landed.at[everything], landed.at[everything], rs_send).wait()
    pltpu.make_async_copy(landed.at[everything], landed.at[everything], ag_send).wait()
    show.wait_send()


def backward_kernel(factor, field_in, target, at, wb, dtr, dti, grad_ref, field_out, v_ref):
    cols = grad_ref.shape[1]
    i = pl.program_id(0)

    @pl.when(i == 0)
    def _():
        for d in range(2):
            for p in range(CHIPS):
                lo = 4 * p
                field_out[d, lo // 128, lo % 128 : lo % 128 + 4, :] = field_in[d, p]
            fr, fi = field_out[d, 0], field_out[d, 1]
            excess = 4.0 * factor * (fr * fr + fi * fi - target[d])
            gr, gi = excess * fr, excess * fi
            g = jnp.concatenate(
                [jnp.concatenate([gr, -gi], axis=1), jnp.concatenate([gi, gr], axis=1)], axis=0
            )
            hi = g.astype(BF16)
            lo = (g - hi.astype(F32)).astype(BF16)
            a = at[:, 256 * d : 256 * d + 256]
            v = jnp.dot(a, hi, preferred_element_type=F32) + jnp.dot(
                a, lo, preferred_element_type=F32
            )
            v_ref[:, 256 * d : 256 * d + 256] = v.astype(BF16)

    rows = grad_ref.shape[0]
    part = pl.ds(pl.multiple_of(i * rows, rows), rows)
    v = v_ref[part, :]
    wide = 256
    for n in range(cols // wide):
        lanes = slice(n * wide, (n + 1) * wide)
        hr = jnp.dot(v, wb[:, lanes], preferred_element_type=F32)
        hi = jnp.dot(
            v, wb[:, cols + n * wide : cols + (n + 1) * wide], preferred_element_type=F32
        )
        grad_ref[:, lanes] = dtr[part, lanes] * hr - dti[part, lanes] * hi


def body(design, coefficients, focal_steps, target):
    rows, cols = design.shape
    total = rows * lax.axis_size("row")
    focal = target.shape[1]
    vmem = pl.BlockSpec(memory_space=pltpu.VMEM)
    smem = pl.BlockSpec(memory_space=pltpu.SMEM)
    dma = pltpu.SemaphoreType.DMA
    field, dtr, dti, at, wb = pl.pallas_call(
        functools.partial(forward_kernel, total),
        out_shape=(
            pltpu.VMEM((2, CHIPS, 4, 128), F32),
            pltpu.VMEM((rows, cols), F32),
            pltpu.VMEM((rows, cols), F32),
            pltpu.VMEM((rows, 512), BF16),
            pltpu.VMEM((512, 2 * cols), BF16),
        ),
        in_specs=[pl.BlockSpec(memory_space=pl.ANY), smem, smem],
        out_specs=(vmem,) * 5,
        scratch_shapes=[
            pltpu.VMEM((rows, cols), F32),
            pltpu.VMEM((CHUNK, 2 * cols), BF16),
            pltpu.VMEM((CHUNK, 2 * cols), BF16),
            pltpu.VMEM((2 * cols, 512), BF16),
            pltpu.VMEM((512, rows), BF16),
            pltpu.VMEM((rows, 512), BF16),
            pltpu.VMEM((rows, 512), BF16),
            pltpu.VMEM((256, 128), F32),
            pltpu.VMEM((256, 128), F32),
            pltpu.VMEM((CHIPS, 4, 128), F32),
            pltpu.VMEM((CHIPS, 4, 128), F32),
            dma((rows // CHUNK,)),
            dma((2,)),
            dma((2,)),
            dma,
            dma,
            dma,
            dma,
        ],
        compiler_params=pltpu.CompilerParams(
            collective_id=0, has_side_effects=True, vmem_limit_bytes=36 * 2**20
        ),
        name="forward",
    )(design, coefficients, focal_steps)

    factor = math.sqrt(total * total) / (4.0 * focal)
    step_rows = 256
    gradient, field = pl.pallas_call(
        functools.partial(backward_kernel, factor),
        grid=(rows // step_rows,),
        out_shape=(
            jax.ShapeDtypeStruct((rows, cols), F32),
            jax.ShapeDtypeStruct((2, 2, focal, focal), F32),
        ),
        in_specs=[vmem] * 6,
        out_specs=(
            pl.BlockSpec((step_rows, cols), lambda i: (i, 0)),
            pl.BlockSpec((2, 2, focal, focal), lambda i: (0, 0, 0, 0)),
        ),
        scratch_shapes=[pltpu.VMEM((rows, 512), BF16)],
        compiler_params=pltpu.CompilerParams(vmem_limit_bytes=20 * 2**20),
        name="backward",
    )(field, target, at, wb, dtr, dti)
    return gradient, field


def solution(mesh):
    return jax.shard_map(
        body,
        mesh=mesh,
        in_specs=(P("row", "col"), P(), P(), P()),
        out_specs=(P("row", "col"), P()),
        check_vma=False,
    )
```

```python
import functools
import math

import jax
import jax.numpy as jnp
from jax import lax
from jax.experimental import pallas as pl
from jax.experimental.pallas import tpu as pltpu
from jax.sharding import PartitionSpec as P

MESH = pl.DeviceIdType.MESH
F32, BF16 = jnp.float32, jnp.bfloat16
AXIS = 4
CHIPS = 64
CHUNK = 256
MROWS = 512


def hops(off):
    return sum(min(a, AXIS - a) for a in off)


OFFSETS = sorted(
    (
        (a, b, c)
        for a in range(AXIS)
        for b in range(AXIS)
        for c in range(AXIS)
        if (a, b, c) != (0, 0, 0)
    ),
    key=lambda off: -hops(off),
)


def coords():
    row, col = lax.axis_index("row"), lax.axis_index("col")
    x, y_lo = lax.rem(row, 4), lax.div(row, 4)
    core, y_hi, z = lax.rem(col, 2), lax.rem(lax.div(col, 2), 2), lax.div(col, 4)
    return x, y_hi * 2 + y_lo, z, core


def device(x, y, z, core):
    return (lax.rem(y, 2) * 4 + x, (z * 2 + lax.div(y, 2)) * 2 + core)


def monomials(c):
    return [
        c[0] - c[2] + c[4] - c[6],
        c[1] - 3.0 * c[3] + 5.0 * c[5] - 7.0 * c[7],
        2.0 * c[2] - 8.0 * c[4] + 18.0 * c[6],
        4.0 * c[3] - 20.0 * c[5] + 56.0 * c[7],
        8.0 * c[4] - 48.0 * c[6],
        16.0 * c[5] - 112.0 * c[7],
        32.0 * c[6],
        64.0 * c[7],
    ]


def horner(x, coefs):
    acc = coefs[-1] * x + coefs[-2]
    for c in coefs[-3::-1]:
        acc = acc * x + c
    return acc


def chirp_rows(first, width, total, steps):
    shape = (8, width)
    u = lax.broadcasted_iota(jnp.int32, shape, 1) + first
    r = lax.broadcasted_iota(jnp.int32, shape, 0)
    mask = 2 * total - 1
    step = jnp.where((r & 2) == 0, steps[0], steps[1])
    off = u & mask
    k = (((off * off) & mask) * step) & mask
    k = (k - (r & 1) * (total // 2)) & mask
    p = total // 2 - jnp.minimum(k, 2 * total - k)
    a = p.astype(F32) * (math.pi / total)
    s = a * a
    poly = horner(s, [(-1.0) ** n / math.factorial(2 * n + 1) for n in range(7)])
    return a * poly * (1.0 / math.sqrt(total))


def across(seq, r, width):
    x = jnp.broadcast_to(seq[pl.ds(r, 1), : width + 128], (128, width + 128))
    return pltpu.roll(x, 0, 1, stride=1, stride_axis=0)[:, 128:].astype(BF16)


def down(seq, r, lo):
    x = jnp.broadcast_to(seq[r : r + 1, pl.ds(pl.multiple_of(lo, 128), 256)], (128, 256))
    return pltpu.roll(x, 0, 1, stride=1, stride_axis=0)[:, 128:].astype(BF16)


def forward_kernel(
    total,
    design_hbm,
    coef,
    steps,
    target_hbm,
    field_ref,
    dtr_ref,
    dti_ref,
    at_ref,
    wb_ref,
    target_ref,
    x_ref,
    t_ref,
    wcol,
    rtab,
    qh,
    ql,
    seq,
    partial,
    sib,
    pieces,
    landed,
    load_sem,
    sib_send,
    sib_recv,
    rs_send,
    rs_recv,
    ag_send,
    ag_recv,
):
    rows, cols = x_ref.shape
    chunks = rows // CHUNK
    x, y, z, core = coords()
    chip = (x * AXIS + y) * AXIS + z
    other = 1 - core
    sibling = device(x, y, z, other)

    def load(i):
        part = pl.ds(pl.multiple_of(i * CHUNK, CHUNK), CHUNK)
        return pltpu.make_async_copy(design_hbm.at[part], x_ref.at[part], load_sem.at[i])

    for i in range(chunks):
        load(i).start()
    fetch = pltpu.make_async_copy(target_hbm, target_ref, load_sem.at[chunks])
    fetch.start()

    xs = [lax.rem(x + a, AXIS) for a in range(AXIS)]
    ys = [lax.rem(y + a, AXIS) for a in range(AXIS)]
    zs = [lax.rem(z + a, AXIS) for a in range(AXIS)]
    y_row = [lax.rem(a, 2) * AXIS for a in ys]
    y_col = [lax.div(a, 2) * 2 + core for a in ys]
    peers = [
        (
            xs[a] * (AXIS * AXIS) + ys[b] * AXIS + zs[c],
            (y_row[b] + xs[a], zs[c] * AXIS + y_col[b]),
        )
        for a, b, c in OFFSETS
    ]

    barrier = pltpu.get_barrier_semaphore()
    pl.semaphore_signal(barrier, inc=1, device_id=sibling, device_id_type=MESH)

    for _, dev in peers:
        pl.semaphore_signal(barrier, inc=1, device_id=dev, device_id_type=MESH)

    step = [steps[0], steps[1]]
    first_row = lax.axis_index("row") * rows - (total // 2 - 64)
    first_col = lax.axis_index("col") * cols - (total // 2 - 64)
    mono = [monomials([coef[i, k] for k in range(8)]) for i in range(2)]

    seq[:, : cols + 128] = chirp_rows(-first_col - cols, cols + 128, total, step)

    @pl.loop(0, cols // 128)
    def _(b):
        upper = pl.ds(pl.multiple_of(b * 128, 128), 128)
        lower = pl.ds(pl.multiple_of(cols + b * 128, 128), 128)
        lo = cols - 128 - b * 128
        for d in range(2):
            re, im = down(seq, 2 * d, lo), down(seq, 2 * d + 1, lo)
            wcol[upper, 256 * d : 256 * d + 128] = re
            wcol[upper, 256 * d + 128 : 256 * d + 256] = im
            wcol[lower, 256 * d : 256 * d + 128] = -im
            wcol[lower, 256 * d + 128 : 256 * d + 256] = re

    seq[...] = chirp_rows(first_row - 128, rows + 128, total, step)

    @pl.loop(0, 4)
    def _(r):
        rtab[pl.ds(pl.multiple_of(128 * r, 128), 128), :] = across(seq, r, rows)

    @pl.loop(0, chunks)
    def _(i):
        load(i).wait()

        @pl.loop(0, CHUNK // 32)
        def _(j):
            part = pl.ds(pl.multiple_of(i * CHUNK + j * 32, 32), 32)
            v = x_ref[part]
            t_ref[part, :cols] = horner(v, mono[0]).astype(BF16)
            t_ref[part, cols:] = horner(v, mono[1]).astype(BF16)

    @pl.loop(0, rows // MROWS)
    def _(i):
        part = pl.ds(pl.multiple_of(i * MROWS, MROWS), MROWS)
        q = jnp.dot(t_ref[part], wcol[...], preferred_element_type=F32)
        hi = q.astype(BF16)
        qh[part] = hi
        ql[part] = (q - hi.astype(F32)).astype(BF16)

    pl.semaphore_wait(barrier, CHIPS)
    give = pltpu.make_async_remote_copy(
        src_ref=partial.at[0],
        dst_ref=sib,
        send_sem=sib_send.at[0],
        recv_sem=sib_recv.at[0],
        device_id=sibling,
        device_id_type=MESH,
    )

    @pl.loop(0, 2)
    def _(i):
        d = other + i * (2 * core - 1)
        a = rtab[pl.ds(pl.multiple_of(d * 256, 256), 256), :]
        lanes = pl.ds(pl.multiple_of(d * 256, 256), 256)
        f = jnp.dot(a, qh[:, lanes], preferred_element_type=F32) + jnp.dot(
            a, ql[:, lanes], preferred_element_type=F32
        )
        partial[i, :128] = f[:128, :128] - f[128:, 128:]
        partial[i, 128:] = f[:128, 128:] + f[128:, :128]

        @pl.when(i == 0)
        def _():
            give.start()

    fetch.wait()
    give.wait_recv()
    total_chip = partial[1] + sib[...]
    for p in range(CHIPS):
        pieces[p] = total_chip[4 * p : 4 * p + 4, :]

    for n, (there, dev) in enumerate(peers):
        pltpu.make_async_remote_copy(
            src_ref=pieces.at[there],
            dst_ref=landed.at[n],
            send_sem=rs_send,
            recv_sem=rs_recv,
            device_id=dev,
            device_id_type=MESH,
        ).start()

    slopes = [[k * m[k] for k in range(1, 8)] for m in mono]

    @pl.loop(0, rows // 32)
    def _(i):
        part = pl.ds(pl.multiple_of(i * 32, 32), 32)
        v = x_ref[part]
        dtr_ref[part] = horner(v, slopes[0])
        dti_ref[part] = horner(v, slopes[1])

    everything = pl.ds(0, CHIPS - 1)
    pltpu.make_async_copy(landed.at[everything], landed.at[everything], rs_recv).wait()
    total_piece = pieces[chip]
    for n in range(CHIPS - 1):
        total_piece = total_piece + landed[n]
    mine = field_ref.at[core]
    mine[chip] = total_piece

    for _, dev in peers:
        pltpu.make_async_remote_copy(
            src_ref=mine.at[chip],
            dst_ref=mine.at[chip],
            send_sem=ag_send,
            recv_sem=ag_recv,
            device_id=dev,
            device_id_type=MESH,
        ).start()

    seq[...] = chirp_rows(-first_row - rows, rows + 128, total, step)

    @pl.loop(0, rows // 128)
    def _(b):
        part = pl.ds(pl.multiple_of(b * 128, 128), 128)
        for r in range(4):
            at_ref[part, 128 * r : 128 * r + 128] = down(seq, r, rows - 128 - b * 128)

    seq[:, : cols + 128] = chirp_rows(first_col - 128, cols + 128, total, step)

    @pl.loop(0, 2)
    def _(d):
        re, im = across(seq, 2 * d, cols), across(seq, 2 * d + 1, cols)
        upper = pl.ds(pl.multiple_of(256 * d, 128), 128)
        lower = pl.ds(pl.multiple_of(256 * d + 128, 128), 128)
        wb_ref[upper, :cols] = re
        wb_ref[upper, cols:] = im
        wb_ref[lower, :cols] = -im
        wb_ref[lower, cols:] = re

    pltpu.make_async_copy(mine.at[everything], mine.at[everything], ag_recv).wait()
    show = pltpu.make_async_remote_copy(
        src_ref=mine,
        dst_ref=field_ref.at[core],
        send_sem=sib_send.at[1],
        recv_sem=sib_recv.at[1],
        device_id=sibling,
        device_id_type=MESH,
    )
    show.start()
    show.wait_recv()
    give.wait_send()
    pltpu.make_async_copy(landed.at[everything], landed.at[everything], rs_send).wait()
    pltpu.make_async_copy(landed.at[everything], landed.at[everything], ag_send).wait()
    show.wait_send()


def backward_kernel(factor, field_in, target, at, wb, dtr, dti, grad_ref, field_out, v_ref, g_ref):
    rows, cols = dtr.shape
    i = pl.program_id(0)

    @pl.when(i == 0)
    def _():
        for d in range(2):
            for p in range(CHIPS):
                lo = 4 * p
                field_out[d, lo // 128, lo % 128 : lo % 128 + 4, :] = field_in[d, p]
            fr, fi = field_out[d, 0], field_out[d, 1]
            excess = 4.0 * factor * (fr * fr + fi * fi - target[d])
            gr, gi = excess * fr, excess * fi
            g_ref[d] = jnp.concatenate(
                [jnp.concatenate([gr, -gi], axis=1), jnp.concatenate([gi, gr], axis=1)], axis=0
            ).astype(BF16)

        @pl.loop(0, rows // MROWS)
        def _(j):
            part = pl.ds(pl.multiple_of(j * MROWS, MROWS), MROWS)
            for d in range(2):
                v = jnp.dot(
                    at[part, 256 * d : 256 * d + 256], g_ref[d], preferred_element_type=F32
                )
                v_ref[part, 256 * d : 256 * d + 256] = v.astype(BF16)

    height = grad_ref.shape[0]
    part = pl.ds(pl.multiple_of(i * height, height), height)
    v = v_ref[part, :]
    for n in range(cols // 256):
        left = slice(n * 256, (n + 1) * 256)
        right = slice(cols + n * 256, cols + (n + 1) * 256)
        hr = jnp.dot(v, wb[:, left], preferred_element_type=F32)
        hi = jnp.dot(v, wb[:, right], preferred_element_type=F32)
        grad_ref[:, left] = dtr[part, left] * hr - dti[part, left] * hi


def body(design, coefficients, focal_steps, target):
    rows, cols = design.shape
    total = rows * lax.axis_size("row")
    focal = target.shape[1]
    vmem = pl.BlockSpec(memory_space=pltpu.VMEM)
    smem = pl.BlockSpec(memory_space=pltpu.SMEM)
    dma = pltpu.SemaphoreType.DMA
    field, dtr, dti, at, wb, target = pl.pallas_call(
        functools.partial(forward_kernel, total),
        out_shape=(
            pltpu.VMEM((2, CHIPS, 4, 128), F32),
            pltpu.VMEM((rows, cols), F32),
            pltpu.VMEM((rows, cols), F32),
            pltpu.VMEM((rows, 512), BF16),
            pltpu.VMEM((512, 2 * cols), BF16),
            pltpu.VMEM(target.shape, F32),
        ),
        in_specs=[pl.BlockSpec(memory_space=pl.ANY), smem, smem, pl.BlockSpec(memory_space=pl.ANY)],
        out_specs=(vmem,) * 6,
        scratch_shapes=[
            pltpu.VMEM((rows, cols), F32),
            pltpu.VMEM((rows, 2 * cols), BF16),
            pltpu.VMEM((2 * cols, 512), BF16),
            pltpu.VMEM((512, rows), BF16),
            pltpu.VMEM((rows, 512), BF16),
            pltpu.VMEM((rows, 512), BF16),
            pltpu.VMEM((8, rows + 128), F32),
            pltpu.VMEM((2, 256, 128), F32),
            pltpu.VMEM((256, 128), F32),
            pltpu.VMEM((CHIPS, 4, 128), F32),
            pltpu.VMEM((CHIPS, 4, 128), F32),
            dma((rows // CHUNK + 1,)),
            dma((2,)),
            dma((2,)),
            dma,
            dma,
            dma,
            dma,
        ],
        compiler_params=pltpu.CompilerParams(
            collective_id=0, has_side_effects=True, vmem_limit_bytes=30 * 2**20
        ),
        name="forward",
    )(design, coefficients, focal_steps, target)

    factor = math.sqrt(total * total) / (4.0 * focal)
    height = MROWS
    gradient, field = pl.pallas_call(
        functools.partial(backward_kernel, factor),
        grid=(rows // height,),
        out_shape=(
            jax.ShapeDtypeStruct((rows, cols), F32),
            jax.ShapeDtypeStruct((2, 2, focal, focal), F32),
        ),
        in_specs=[vmem] * 6,
        out_specs=(
            pl.BlockSpec((height, cols), lambda i: (i, 0)),
            pl.BlockSpec((2, 2, focal, focal), lambda i: (0, 0, 0, 0)),
        ),
        scratch_shapes=[pltpu.VMEM((rows, 512), BF16), pltpu.VMEM((2, 256, 256), BF16)],
        compiler_params=pltpu.CompilerParams(vmem_limit_bytes=14 * 2**20),
        name="backward",
    )(field, target, at, wb, dtr, dti)
    return gradient, field


def solution(mesh):
    return jax.shard_map(
        body,
        mesh=mesh,
        in_specs=(P("row", "col"), P(), P(), P()),
        out_specs=(P("row", "col"), P()),
        check_vma=False,
    )
```

```python
import functools
import math

import jax
import jax.numpy as jnp
from jax import lax
from jax.experimental import pallas as pl
from jax.experimental.pallas import tpu as pltpu
from jax.sharding import PartitionSpec as P

MESH = pl.DeviceIdType.MESH
F32, BF16 = jnp.float32, jnp.bfloat16
AXIS = 4
CHIPS = 64
CHUNK = 256
MROWS = 512


def hops(off):
    return sum(min(a, AXIS - a) for a in off)


OFFSETS = sorted(
    (
        (a, b, c)
        for a in range(AXIS)
        for b in range(AXIS)
        for c in range(AXIS)
        if (a, b, c) != (0, 0, 0)
    ),
    key=lambda off: -hops(off),
)


def coords():
    row, col = lax.axis_index("row"), lax.axis_index("col")
    x, y_lo = lax.rem(row, 4), lax.div(row, 4)
    core, y_hi, z = lax.rem(col, 2), lax.rem(lax.div(col, 2), 2), lax.div(col, 4)
    return x, y_hi * 2 + y_lo, z, core


def device(x, y, z, core):
    return (lax.rem(y, 2) * 4 + x, (z * 2 + lax.div(y, 2)) * 2 + core)


def monomials(c):
    return [
        c[0] - c[2] + c[4] - c[6],
        c[1] - 3.0 * c[3] + 5.0 * c[5] - 7.0 * c[7],
        2.0 * c[2] - 8.0 * c[4] + 18.0 * c[6],
        4.0 * c[3] - 20.0 * c[5] + 56.0 * c[7],
        8.0 * c[4] - 48.0 * c[6],
        16.0 * c[5] - 112.0 * c[7],
        32.0 * c[6],
        64.0 * c[7],
    ]


def horner(x, coefs):
    acc = coefs[-1] * x + coefs[-2]
    for c in coefs[-3::-1]:
        acc = acc * x + c
    return acc


def chirp_rows(first, width, total, steps):
    shape = (8, width)
    u = lax.broadcasted_iota(jnp.int32, shape, 1) + first
    r = lax.broadcasted_iota(jnp.int32, shape, 0)
    mask = 2 * total - 1
    step = jnp.where((r & 2) == 0, steps[0], steps[1])
    off = u & mask
    k = (((off * off) & mask) * step) & mask
    k = (k - (r & 1) * (total // 2)) & mask
    p = total // 2 - jnp.minimum(k, 2 * total - k)
    a = p.astype(F32) * (math.pi / total)
    s = a * a
    poly = horner(s, [(-1.0) ** n / math.factorial(2 * n + 1) for n in range(7)])
    return a * poly * (1.0 / math.sqrt(total))


def across(seq, r, width):
    x = jnp.broadcast_to(seq[pl.ds(r, 1), : width + 128], (128, width + 128))
    return pltpu.roll(x, 0, 1, stride=1, stride_axis=0)[:, 128:].astype(BF16)


def down(seq, r, lo):
    x = jnp.broadcast_to(seq[r : r + 1, pl.ds(pl.multiple_of(lo, 128), 256)], (128, 256))
    return pltpu.roll(x, 0, 1, stride=1, stride_axis=0)[:, 128:].astype(BF16)


def forward_kernel(
    total,
    design_hbm,
    coef_hbm,
    steps_hbm,
    target_hbm,
    field_ref,
    dtr_ref,
    dti_ref,
    at_ref,
    wb_ref,
    target_ref,
    coef,
    steps,
    x_ref,
    t0,
    t1,
    wcol,
    rtab,
    qh,
    ql,
    seq,
    partial,
    sib,
    pieces,
    landed,
    load_sem,
    sib_send,
    sib_recv,
    rs_send,
    rs_recv,
    ag_send,
    ag_recv,
):
    rows, cols = x_ref.shape
    chunks = rows // CHUNK
    x, y, z, core = coords()
    chip = (x * AXIS + y) * AXIS + z
    other = 1 - core
    sibling = device(x, y, z, other)

    def load(i):
        part = pl.ds(pl.multiple_of(i * CHUNK, CHUNK), CHUNK)
        return pltpu.make_async_copy(design_hbm.at[part], x_ref.at[part], load_sem.at[i])

    fetches = [
        pltpu.make_async_copy(src, dst, load_sem.at[chunks + 1 + n])
        for n, (src, dst) in enumerate([(steps_hbm, steps), (coef_hbm, coef)])
    ]
    for fetch in fetches:
        fetch.start()
    for i in range(chunks):
        load(i).start()
    fetch = pltpu.make_async_copy(target_hbm, target_ref, load_sem.at[chunks])
    fetch.start()

    xs = [lax.rem(x + a, AXIS) for a in range(AXIS)]
    ys = [lax.rem(y + a, AXIS) for a in range(AXIS)]
    zs = [lax.rem(z + a, AXIS) for a in range(AXIS)]
    y_row = [lax.rem(a, 2) * AXIS for a in ys]
    y_col = [lax.div(a, 2) * 2 + core for a in ys]
    peers = [
        (
            xs[a] * (AXIS * AXIS) + ys[b] * AXIS + zs[c],
            (y_row[b] + xs[a], zs[c] * AXIS + y_col[b]),
        )
        for a, b, c in OFFSETS
    ]

    barrier = pltpu.get_barrier_semaphore()
    pl.semaphore_signal(barrier, inc=1, device_id=sibling, device_id_type=MESH)

    for _, dev in peers:
        pl.semaphore_signal(barrier, inc=1, device_id=dev, device_id_type=MESH)

    for ready in fetches:
        ready.wait()
    step = [steps[0], steps[1]]
    first_row = lax.axis_index("row") * rows - (total // 2 - 64)
    first_col = lax.axis_index("col") * cols - (total // 2 - 64)
    mono = [monomials([coef[i, k] for k in range(8)]) for i in range(2)]

    seq[:, : cols + 128] = chirp_rows(-first_col - cols, cols + 128, total, step)

    @pl.loop(0, cols // 128)
    def _(b):
        upper = pl.ds(pl.multiple_of(b * 128, 128), 128)
        lower = pl.ds(pl.multiple_of(cols + b * 128, 128), 128)
        lo = cols - 128 - b * 128
        for d in range(2):
            re, im = down(seq, 2 * d, lo), down(seq, 2 * d + 1, lo)
            wcol[upper, 256 * d : 256 * d + 128] = re
            wcol[upper, 256 * d + 128 : 256 * d + 256] = im
            wcol[lower, 256 * d : 256 * d + 128] = -im
            wcol[lower, 256 * d + 128 : 256 * d + 256] = re

    seq[...] = chirp_rows(first_row - 128, rows + 128, total, step)

    @pl.loop(0, 4)
    def _(r):
        rtab[pl.ds(pl.multiple_of(128 * r, 128), 128), :] = across(seq, r, rows)

    def transmit(i, t):
        v = x_ref[pl.ds(pl.multiple_of(i * CHUNK, CHUNK), CHUNK)]
        t[:, :cols] = horner(v, mono[0]).astype(BF16)
        t[:, cols:] = horner(v, mono[1]).astype(BF16)

    def contract(i, t):
        part = pl.ds(pl.multiple_of(i * CHUNK, CHUNK), CHUNK)
        q = jnp.dot(t[...], wcol[...], preferred_element_type=F32)
        hi = q.astype(BF16)
        qh[part] = hi
        ql[part] = (q - hi.astype(F32)).astype(BF16)

    load(0).wait()
    transmit(0, t0)
    for i in range(1, chunks):
        load(i).wait()

    @pl.loop(0, chunks // 2 - 1)
    def _(k):
        transmit(2 * k + 1, t1)
        contract(2 * k, t0)
        transmit(2 * k + 2, t0)
        contract(2 * k + 1, t1)

    transmit(chunks - 1, t1)
    contract(chunks - 2, t0)
    contract(chunks - 1, t1)

    pl.semaphore_wait(barrier, CHIPS)
    give = pltpu.make_async_remote_copy(
        src_ref=partial.at[0],
        dst_ref=sib,
        send_sem=sib_send.at[0],
        recv_sem=sib_recv.at[0],
        device_id=sibling,
        device_id_type=MESH,
    )

    @pl.loop(0, 2)
    def _(i):
        d = other + i * (2 * core - 1)
        a = rtab[pl.ds(pl.multiple_of(d * 256, 256), 256), :]
        lanes = pl.ds(pl.multiple_of(d * 256, 256), 256)
        f = jnp.dot(a, qh[:, lanes], preferred_element_type=F32) + jnp.dot(
            a, ql[:, lanes], preferred_element_type=F32
        )
        partial[i, :128] = f[:128, :128] - f[128:, 128:]
        partial[i, 128:] = f[:128, 128:] + f[128:, :128]

        @pl.when(i == 0)
        def _():
            give.start()

    fetch.wait()
    give.wait_recv()
    total_chip = partial[1] + sib[...]
    for p in range(CHIPS):
        pieces[p] = total_chip[4 * p : 4 * p + 4, :]

    for n, (there, dev) in enumerate(peers):
        pltpu.make_async_remote_copy(
            src_ref=pieces.at[there],
            dst_ref=landed.at[n],
            send_sem=rs_send,
            recv_sem=rs_recv,
            device_id=dev,
            device_id_type=MESH,
        ).start()

    slopes = [[k * m[k] for k in range(1, 8)] for m in mono]

    @pl.loop(0, rows // 32)
    def _(i):
        part = pl.ds(pl.multiple_of(i * 32, 32), 32)
        v = x_ref[part]
        dtr_ref[part] = horner(v, slopes[0])
        dti_ref[part] = horner(v, slopes[1])

    everything = pl.ds(0, CHIPS - 1)
    pltpu.make_async_copy(landed.at[everything], landed.at[everything], rs_recv).wait()
    total_piece = pieces[chip]
    for n in range(CHIPS - 1):
        total_piece = total_piece + landed[n]
    mine = field_ref.at[core]
    mine[chip] = total_piece

    for _, dev in peers:
        pltpu.make_async_remote_copy(
            src_ref=mine.at[chip],
            dst_ref=mine.at[chip],
            send_sem=ag_send,
            recv_sem=ag_recv,
            device_id=dev,
            device_id_type=MESH,
        ).start()

    seq[...] = chirp_rows(-first_row - rows, rows + 128, total, step)

    @pl.loop(0, rows // 128)
    def _(b):
        part = pl.ds(pl.multiple_of(b * 128, 128), 128)
        for r in range(4):
            at_ref[part, 128 * r : 128 * r + 128] = down(seq, r, rows - 128 - b * 128)

    seq[:, : cols + 128] = chirp_rows(first_col - 128, cols + 128, total, step)

    @pl.loop(0, 2)
    def _(d):
        re, im = across(seq, 2 * d, cols), across(seq, 2 * d + 1, cols)
        part = pl.ds(pl.multiple_of(128 * d, 128), 128)
        re32, im32 = re.astype(F32), im.astype(F32)
        wb_ref[0, part] = re
        wb_ref[1, part] = (im32 - re32).astype(BF16)
        wb_ref[2, part] = (im32 + re32).astype(BF16)

    pltpu.make_async_copy(mine.at[everything], mine.at[everything], ag_recv).wait()
    show = pltpu.make_async_remote_copy(
        src_ref=mine,
        dst_ref=field_ref.at[core],
        send_sem=sib_send.at[1],
        recv_sem=sib_recv.at[1],
        device_id=sibling,
        device_id_type=MESH,
    )
    show.start()
    show.wait_recv()
    give.wait_send()
    pltpu.make_async_copy(landed.at[everything], landed.at[everything], rs_send).wait()
    pltpu.make_async_copy(landed.at[everything], landed.at[everything], ag_send).wait()
    show.wait_send()


def backward_kernel(
    factor,
    field_in,
    target,
    at,
    wb,
    dtr,
    dti,
    grad_hbm,
    field_out,
    g_ref,
    vr_ref,
    vi_ref,
    vs_ref,
    out,
    sem,
):
    rows, cols = dtr.shape
    blocks = rows // MROWS
    for d in range(2):
        for p in range(CHIPS):
            lo = 4 * p
            field_out[d, lo // 128, lo % 128 : lo % 128 + 4, :] = field_in[d, p]
        fr, fi = field_out[d, 0], field_out[d, 1]
        excess = 4.0 * factor * (fr * fr + fi * fi - target[d])
        gr, gi = excess * fr, excess * fi
        g_ref[d] = jnp.concatenate(
            [jnp.concatenate([gr, -gi], axis=1), jnp.concatenate([gi, gr], axis=1)], axis=0
        ).astype(BF16)

    @pl.loop(0, blocks)
    def _(j):
        part = pl.ds(pl.multiple_of(j * MROWS, MROWS), MROWS)
        for d in range(2):
            v = jnp.dot(at[part, 256 * d : 256 * d + 256], g_ref[d], preferred_element_type=F32)
            v = v.astype(BF16)
            lanes = slice(128 * d, 128 * d + 128)
            vr_ref[part, lanes] = v[:, :128]
            vi_ref[part, lanes] = v[:, 128:]
            vs_ref[part, lanes] = (v[:, :128].astype(F32) + v[:, 128:].astype(F32)).astype(BF16)

    def write(i, n):
        slot = lax.rem(i, 2)
        lanes = pl.ds(n * 256, 256)
        return pltpu.make_async_copy(
            out.at[slot, :, lanes],
            grad_hbm.at[pl.ds(pl.multiple_of(i * MROWS, MROWS), MROWS), lanes],
            sem.at[slot, n],
        )

    @pl.loop(0, blocks)
    def _(i):
        @pl.when(i >= 2)
        def _():
            for n in range(cols // 256):
                write(i - 2, n).wait()

        part = pl.ds(pl.multiple_of(i * MROWS, MROWS), MROWS)
        slot = lax.rem(i, 2)
        for n in range(cols // 256):
            lanes = slice(n * 256, (n + 1) * 256)
            k1 = jnp.dot(vs_ref[part, :], wb[0, :, lanes], preferred_element_type=F32)
            k2 = jnp.dot(vr_ref[part, :], wb[1, :, lanes], preferred_element_type=F32)
            k3 = jnp.dot(vi_ref[part, :], wb[2, :, lanes], preferred_element_type=F32)
            out[slot, :, lanes] = dtr[part, lanes] * (k1 - k3) - dti[part, lanes] * (k1 + k2)
            write(i, n).start()

    for i in range(blocks - 2, blocks):
        for n in range(cols // 256):
            write(i, n).wait()


def body(design, coefficients, focal_steps, target):
    rows, cols = design.shape
    total = rows * lax.axis_size("row")
    focal = target.shape[1]
    vmem = pl.BlockSpec(memory_space=pltpu.VMEM)
    dma = pltpu.SemaphoreType.DMA
    field, dtr, dti, at, wb, target = pl.pallas_call(
        functools.partial(forward_kernel, total),
        out_shape=(
            pltpu.VMEM((2, CHIPS, 4, 128), F32),
            pltpu.VMEM((rows, cols), F32),
            pltpu.VMEM((rows, cols), F32),
            pltpu.VMEM((rows, 512), BF16),
            pltpu.VMEM((3, 256, cols), BF16),
            pltpu.VMEM(target.shape, F32),
        ),
        in_specs=[pl.BlockSpec(memory_space=pltpu.HBM)] * 4,
        out_specs=(vmem,) * 6,
        scratch_shapes=[
            pltpu.SMEM(coefficients.shape, F32),
            pltpu.SMEM(focal_steps.shape, jnp.int32),
            pltpu.VMEM((rows, cols), F32),
            pltpu.VMEM((CHUNK, 2 * cols), BF16),
            pltpu.VMEM((CHUNK, 2 * cols), BF16),
            pltpu.VMEM((2 * cols, 512), BF16),
            pltpu.VMEM((512, rows), BF16),
            pltpu.VMEM((rows, 512), BF16),
            pltpu.VMEM((rows, 512), BF16),
            pltpu.VMEM((8, rows + 128), F32),
            pltpu.VMEM((2, 256, 128), F32),
            pltpu.VMEM((256, 128), F32),
            pltpu.VMEM((CHIPS, 4, 128), F32),
            pltpu.VMEM((CHIPS, 4, 128), F32),
            dma((rows // CHUNK + 3,)),
            dma((2,)),
            dma((2,)),
            dma,
            dma,
            dma,
            dma,
        ],
        compiler_params=pltpu.CompilerParams(
            collective_id=0, has_side_effects=True, vmem_limit_bytes=30 * 2**20
        ),
        name="forward",
    )(*(pltpu.with_memory_space_constraint(a, pltpu.HBM) for a in (design, coefficients, focal_steps, target)))

    factor = math.sqrt(total * total) / (4.0 * focal)
    gradient, field = pl.pallas_call(
        functools.partial(backward_kernel, factor),
        out_shape=(
            jax.ShapeDtypeStruct((rows, cols), F32),
            jax.ShapeDtypeStruct((2, 2, focal, focal), F32),
        ),
        in_specs=[vmem] * 6,
        out_specs=(pl.BlockSpec(memory_space=pl.ANY), vmem),
        scratch_shapes=[
            pltpu.VMEM((2, 256, 256), BF16),
            pltpu.VMEM((rows, 256), BF16),
            pltpu.VMEM((rows, 256), BF16),
            pltpu.VMEM((rows, 256), BF16),
            pltpu.VMEM((2, MROWS, cols), F32),
            dma((2, cols // 256)),
        ],
        compiler_params=pltpu.CompilerParams(vmem_limit_bytes=14 * 2**20),
        name="backward",
    )(field, target, at, wb, dtr, dti)
    return gradient, field


def solution(mesh):
    return jax.shard_map(
        body,
        mesh=mesh,
        in_specs=(P("row", "col"), P(), P(), P()),
        out_specs=(P("row", "col"), P()),
        check_vma=False,
    )
```

```python
import functools
import math

import jax
import jax.numpy as jnp
from jax import lax
from jax.experimental import pallas as pl
from jax.experimental.pallas import tpu as pltpu
from jax.sharding import PartitionSpec as P

MESH = pl.DeviceIdType.MESH
F32, BF16 = jnp.float32, jnp.bfloat16
AXIS = 4
CHIPS = 64
CHUNK = 256
MROWS = 512


def hops(off):
    return sum(min(a, AXIS - a) for a in off)


OFFSETS = sorted(
    (
        (a, b, c)
        for a in range(AXIS)
        for b in range(AXIS)
        for c in range(AXIS)
        if (a, b, c) != (0, 0, 0)
    ),
    key=lambda off: -hops(off),
)


def coords():
    row, col = lax.axis_index("row"), lax.axis_index("col")
    x, y_lo = lax.rem(row, 4), lax.div(row, 4)
    core, y_hi, z = lax.rem(col, 2), lax.rem(lax.div(col, 2), 2), lax.div(col, 4)
    return x, y_hi * 2 + y_lo, z, core


def device(x, y, z, core):
    return (lax.rem(y, 2) * 4 + x, (z * 2 + lax.div(y, 2)) * 2 + core)


def monomials(c):
    return [
        c[0] - c[2] + c[4] - c[6],
        c[1] - 3.0 * c[3] + 5.0 * c[5] - 7.0 * c[7],
        2.0 * c[2] - 8.0 * c[4] + 18.0 * c[6],
        4.0 * c[3] - 20.0 * c[5] + 56.0 * c[7],
        8.0 * c[4] - 48.0 * c[6],
        16.0 * c[5] - 112.0 * c[7],
        32.0 * c[6],
        64.0 * c[7],
    ]


def horner(x, coefs):
    acc = coefs[-1] * x + coefs[-2]
    for c in coefs[-3::-1]:
        acc = acc * x + c
    return acc


def chirp_rows(first, width, total, steps):
    shape = (8, width)
    u = lax.broadcasted_iota(jnp.int32, shape, 1) + first
    r = lax.broadcasted_iota(jnp.int32, shape, 0)
    mask = 2 * total - 1
    step = jnp.where((r & 2) == 0, steps[0], steps[1])
    off = u & mask
    k = (((off * off) & mask) * step) & mask
    k = (k - (r & 1) * (total // 2)) & mask
    p = total // 2 - jnp.minimum(k, 2 * total - k)
    a = p.astype(F32) * (math.pi / total)
    s = a * a
    poly = horner(s, [(-1.0) ** n / math.factorial(2 * n + 1) for n in range(7)])
    return a * poly * (1.0 / math.sqrt(total))


def across(seq, r, width):
    x = jnp.broadcast_to(seq[pl.ds(r, 1), : width + 128], (128, width + 128))
    return pltpu.roll(x, 0, 1, stride=1, stride_axis=0)[:, 128:].astype(BF16)


def down(seq, r, lo):
    x = jnp.broadcast_to(seq[r : r + 1, pl.ds(pl.multiple_of(lo, 128), 256)], (128, 256))
    return pltpu.roll(x, 0, 1, stride=1, stride_axis=0)[:, 128:].astype(BF16)


def forward_kernel(
    total,
    design_hbm,
    coef_hbm,
    steps_hbm,
    target_hbm,
    field_out,
    dtr_ref,
    dti_ref,
    vr_ref,
    vi_ref,
    vs_ref,
    wb_ref,
    target_ref,
    field_ref,
    at_ref,
    g_ref,
    coef,
    steps,
    x_ref,
    t0,
    t1,
    wcol,
    rtab,
    qh,
    seq,
    row_seq,
    partial,
    sib,
    pieces,
    landed,
    load_sem,
    sib_send,
    sib_recv,
    rs_send,
    rs_recv,
    ag_send,
    ag_recv,
):
    rows, cols = x_ref.shape
    chunks = rows // CHUNK
    x, y, z, core = coords()
    chip = (x * AXIS + y) * AXIS + z
    other = 1 - core
    sibling = device(x, y, z, other)

    def load(i):
        part = pl.ds(pl.multiple_of(i * CHUNK, CHUNK), CHUNK)
        return pltpu.make_async_copy(design_hbm.at[part], x_ref.at[part], load_sem.at[i])

    fetches = [
        pltpu.make_async_copy(src, dst, load_sem.at[chunks + 1 + n])
        for n, (src, dst) in enumerate([(steps_hbm, steps), (coef_hbm, coef)])
    ]
    for fetch in fetches:
        fetch.start()
    for i in range(chunks):
        load(i).start()
    fetch = pltpu.make_async_copy(target_hbm, target_ref, load_sem.at[chunks])
    fetch.start()

    xs = [lax.rem(x + a, AXIS) for a in range(AXIS)]
    ys = [lax.rem(y + a, AXIS) for a in range(AXIS)]
    zs = [lax.rem(z + a, AXIS) for a in range(AXIS)]
    y_row = [lax.rem(a, 2) * AXIS for a in ys]
    y_col = [lax.div(a, 2) * 2 + core for a in ys]
    peers = [
        (
            xs[a] * (AXIS * AXIS) + ys[b] * AXIS + zs[c],
            (y_row[b] + xs[a], zs[c] * AXIS + y_col[b]),
        )
        for a, b, c in OFFSETS
    ]

    barrier = pltpu.get_barrier_semaphore()
    pl.semaphore_signal(barrier, inc=1, device_id=sibling, device_id_type=MESH)

    for _, dev in peers:
        pl.semaphore_signal(barrier, inc=1, device_id=dev, device_id_type=MESH)

    for ready in fetches:
        ready.wait()
    step = [steps[0], steps[1]]
    first_row = lax.axis_index("row") * rows - (total // 2 - 64)
    first_col = lax.axis_index("col") * cols - (total // 2 - 64)
    mono = [monomials([coef[i, k] for k in range(8)]) for i in range(2)]

    seq[:, : cols + 128] = chirp_rows(-first_col - cols, cols + 128, total, step)
    row_seq[...] = chirp_rows(first_row - 128, rows + 128, total, step)

    @pl.loop(0, cols // 128)
    def _(b):
        upper = pl.ds(pl.multiple_of(b * 128, 128), 128)
        lower = pl.ds(pl.multiple_of(cols + b * 128, 128), 128)
        lo = cols - 128 - b * 128
        for d in range(2):
            re, im = down(seq, 2 * d, lo), down(seq, 2 * d + 1, lo)
            wcol[upper, 256 * d : 256 * d + 128] = re
            wcol[upper, 256 * d + 128 : 256 * d + 256] = im
            wcol[lower, 256 * d : 256 * d + 128] = -im
            wcol[lower, 256 * d + 128 : 256 * d + 256] = re

    def row_table(r):
        rtab[pl.ds(pl.multiple_of(128 * r, 128), 128), :] = across(row_seq, r, rows)

    def transmit(i, t):
        v = x_ref[pl.ds(pl.multiple_of(i * CHUNK, CHUNK), CHUNK)]
        t[:, :cols] = horner(v, mono[0]).astype(BF16)
        t[:, cols:] = horner(v, mono[1]).astype(BF16)

    def contract(i, t):
        part = pl.ds(pl.multiple_of(i * CHUNK, CHUNK), CHUNK)
        q = jnp.dot(t[...], wcol[...], preferred_element_type=F32)
        qh[part] = q.astype(BF16)

    load(0).wait()
    transmit(0, t0)
    for i in range(1, chunks):
        load(i).wait()

    @pl.loop(0, chunks // 2 - 1)
    def _(k):
        row_table(k)
        transmit(2 * k + 1, t1)
        contract(2 * k, t0)
        transmit(2 * k + 2, t0)
        contract(2 * k + 1, t1)

    row_table(3)
    transmit(chunks - 1, t1)
    contract(chunks - 2, t0)
    contract(chunks - 1, t1)

    pl.semaphore_wait(barrier, CHIPS)
    give = pltpu.make_async_remote_copy(
        src_ref=partial.at[0],
        dst_ref=sib,
        send_sem=sib_send.at[0],
        recv_sem=sib_recv.at[0],
        device_id=sibling,
        device_id_type=MESH,
    )

    @pl.loop(0, 2)
    def _(i):
        d = other + i * (2 * core - 1)
        a = rtab[pl.ds(pl.multiple_of(d * 256, 256), 256), :]
        lanes = pl.ds(pl.multiple_of(d * 256, 256), 256)
        f = jnp.dot(a, qh[:, lanes], preferred_element_type=F32)
        partial[i, :128] = f[:128, :128] - f[128:, 128:]
        partial[i, 128:] = f[:128, 128:] + f[128:, :128]

        @pl.when(i == 0)
        def _():
            give.start()

    fetch.wait()
    give.wait_recv()
    total_chip = partial[1] + sib[...]
    for p in range(CHIPS):
        pieces[p] = total_chip[4 * p : 4 * p + 4, :]

    for n, (there, dev) in enumerate(peers):
        pltpu.make_async_remote_copy(
            src_ref=pieces.at[there],
            dst_ref=landed.at[n],
            send_sem=rs_send,
            recv_sem=rs_recv,
            device_id=dev,
            device_id_type=MESH,
        ).start()

    slopes = [[k * m[k] for k in range(1, 8)] for m in mono]

    @pl.loop(0, rows // 32)
    def _(i):
        part = pl.ds(pl.multiple_of(i * 32, 32), 32)
        v = x_ref[part]
        dtr_ref[part] = horner(v, slopes[0])
        dti_ref[part] = horner(v, slopes[1])

    everything = pl.ds(0, CHIPS - 1)
    pltpu.make_async_copy(landed.at[everything], landed.at[everything], rs_recv).wait()
    total_piece = pieces[chip]
    for n in range(CHIPS - 1):
        total_piece = total_piece + landed[n]
    mine = field_ref.at[core]
    mine[chip] = total_piece

    for _, dev in peers:
        pltpu.make_async_remote_copy(
            src_ref=mine.at[chip],
            dst_ref=mine.at[chip],
            send_sem=ag_send,
            recv_sem=ag_recv,
            device_id=dev,
            device_id_type=MESH,
        ).start()

    seq[...] = chirp_rows(-first_row - rows, rows + 128, total, step)

    @pl.loop(0, rows // 128)
    def _(b):
        part = pl.ds(pl.multiple_of(b * 128, 128), 128)
        for r in range(4):
            at_ref[part, 128 * r : 128 * r + 128] = down(seq, r, rows - 128 - b * 128)

    seq[:, : cols + 128] = chirp_rows(first_col - 128, cols + 128, total, step)

    @pl.loop(0, 2)
    def _(d):
        re, im = across(seq, 2 * d, cols), across(seq, 2 * d + 1, cols)
        part = pl.ds(pl.multiple_of(128 * d, 128), 128)
        re32, im32 = re.astype(F32), im.astype(F32)
        wb_ref[0, part] = re
        wb_ref[1, part] = (im32 - re32).astype(BF16)
        wb_ref[2, part] = (im32 + re32).astype(BF16)

    pltpu.make_async_copy(mine.at[everything], mine.at[everything], ag_recv).wait()
    show = pltpu.make_async_remote_copy(
        src_ref=mine,
        dst_ref=field_ref.at[core],
        send_sem=sib_send.at[1],
        recv_sem=sib_recv.at[1],
        device_id=sibling,
        device_id_type=MESH,
    )
    show.start()

    factor = math.sqrt(total * total) / (4.0 * 128)

    @pl.loop(0, 2)
    def _(i):
        d = core + i * (1 - 2 * core)

        @pl.when(i == 1)
        def _():
            show.wait_recv()

        for p in range(CHIPS):
            lo = 4 * p
            field_out[d, lo // 128, lo % 128 : lo % 128 + 4, :] = field_ref[d, p]
        fr, fi = field_out[d, 0], field_out[d, 1]
        excess = 4.0 * factor * (fr * fr + fi * fi - target_ref[d])
        gr, gi = excess * fr, excess * fi
        g_ref[...] = jnp.concatenate(
            [jnp.concatenate([gr, -gi], axis=1), jnp.concatenate([gi, gr], axis=1)], axis=0
        ).astype(BF16)
        near = pl.ds(pl.multiple_of(256 * d, 256), 256)
        lanes = pl.ds(pl.multiple_of(128 * d, 128), 128)

        @pl.loop(0, rows // MROWS)
        def _(j):
            part = pl.ds(pl.multiple_of(j * MROWS, MROWS), MROWS)
            v = jnp.dot(at_ref[part, near], g_ref[...], preferred_element_type=F32).astype(BF16)
            vr_ref[part, lanes] = v[:, :128]
            vi_ref[part, lanes] = v[:, 128:]
            vs_ref[part, lanes] = (v[:, :128].astype(F32) + v[:, 128:].astype(F32)).astype(BF16)

    give.wait_send()
    pltpu.make_async_copy(landed.at[everything], landed.at[everything], rs_send).wait()
    pltpu.make_async_copy(landed.at[everything], landed.at[everything], ag_send).wait()
    show.wait_send()


def backward_kernel(
    field, vr_ref, vi_ref, vs_ref, wb, dtr, dti, grad_hbm, field_hbm, out, sem, field_sem
):
    rows, cols = dtr.shape
    blocks = rows // MROWS
    show = pltpu.make_async_copy(field, field_hbm, field_sem)
    show.start()

    def write(i, n):
        slot = lax.rem(i, 2)
        lanes = pl.ds(n * 256, 256)
        return pltpu.make_async_copy(
            out.at[slot, :, lanes],
            grad_hbm.at[pl.ds(pl.multiple_of(i * MROWS, MROWS), MROWS), lanes],
            sem.at[slot, n],
        )

    @pl.loop(0, blocks)
    def _(i):
        @pl.when(i >= 2)
        def _():
            for n in range(cols // 256):
                write(i - 2, n).wait()

        part = pl.ds(pl.multiple_of(i * MROWS, MROWS), MROWS)
        slot = lax.rem(i, 2)
        for n in range(cols // 256):
            lanes = slice(n * 256, (n + 1) * 256)
            k1 = jnp.dot(vs_ref[part, :], wb[0, :, lanes], preferred_element_type=F32)
            k2 = jnp.dot(vr_ref[part, :], wb[1, :, lanes], preferred_element_type=F32)
            k3 = jnp.dot(vi_ref[part, :], wb[2, :, lanes], preferred_element_type=F32)
            out[slot, :, lanes] = dtr[part, lanes] * (k1 - k3) - dti[part, lanes] * (k1 + k2)
            write(i, n).start()

    for i in range(blocks - 2, blocks):
        for n in range(cols // 256):
            write(i, n).wait()
    show.wait()


def body(design, coefficients, focal_steps, target):
    rows, cols = design.shape
    total = rows * lax.axis_size("row")
    focal = target.shape[1]
    vmem = pl.BlockSpec(memory_space=pltpu.VMEM)
    dma = pltpu.SemaphoreType.DMA
    half = pltpu.VMEM((rows, 256), BF16)
    field, dtr, dti, vr, vi, vs, wb = pl.pallas_call(
        functools.partial(forward_kernel, total),
        out_shape=(
            pltpu.VMEM((2, 2, focal, focal), F32),
            pltpu.VMEM((rows, cols), F32),
            pltpu.VMEM((rows, cols), F32),
            half,
            half,
            half,
            pltpu.VMEM((3, 256, cols), BF16),
        ),
        in_specs=[pl.BlockSpec(memory_space=pltpu.HBM)] * 4,
        out_specs=(vmem,) * 7,
        scratch_shapes=[
            pltpu.VMEM(target.shape, F32),
            pltpu.VMEM((2, CHIPS, 4, 128), F32),
            pltpu.VMEM((rows, 512), BF16),
            pltpu.VMEM((256, 256), BF16),
            pltpu.SMEM(coefficients.shape, F32),
            pltpu.SMEM(focal_steps.shape, jnp.int32),
            pltpu.VMEM((rows, cols), F32),
            pltpu.VMEM((CHUNK, 2 * cols), BF16),
            pltpu.VMEM((CHUNK, 2 * cols), BF16),
            pltpu.VMEM((2 * cols, 512), BF16),
            pltpu.VMEM((512, rows), BF16),
            pltpu.VMEM((rows, 512), BF16),
            pltpu.VMEM((8, rows + 128), F32),
            pltpu.VMEM((8, rows + 128), F32),
            pltpu.VMEM((2, 256, 128), F32),
            pltpu.VMEM((256, 128), F32),
            pltpu.VMEM((CHIPS, 4, 128), F32),
            pltpu.VMEM((CHIPS, 4, 128), F32),
            dma((rows // CHUNK + 3,)),
            dma((2,)),
            dma((2,)),
            dma,
            dma,
            dma,
            dma,
        ],
        compiler_params=pltpu.CompilerParams(
            collective_id=0, has_side_effects=True, vmem_limit_bytes=30 * 2**20
        ),
        name="forward",
    )(*(pltpu.with_memory_space_constraint(a, pltpu.HBM) for a in (design, coefficients, focal_steps, target)))

    anywhere = pl.BlockSpec(memory_space=pl.ANY)
    gradient, field = pl.pallas_call(
        backward_kernel,
        out_shape=(
            jax.ShapeDtypeStruct((rows, cols), F32),
            jax.ShapeDtypeStruct((2, 2, focal, focal), F32),
        ),
        in_specs=[vmem] * 7,
        out_specs=(anywhere, anywhere),
        scratch_shapes=[
            pltpu.VMEM((2, MROWS, cols), F32),
            dma((2, cols // 256)),
            dma,
        ],
        compiler_params=pltpu.CompilerParams(vmem_limit_bytes=10 * 2**20),
        name="backward",
    )(field, vr, vi, vs, wb, dtr, dti)
    return gradient, field


def solution(mesh):
    return jax.shard_map(
        body,
        mesh=mesh,
        in_specs=(P("row", "col"), P(), P(), P()),
        out_specs=(P("row", "col"), P()),
        check_vma=False,
    )
```

```python
import functools
import math

import jax
import jax.numpy as jnp
from jax import lax
from jax.experimental import pallas as pl
from jax.experimental.pallas import tpu as pltpu
from jax.sharding import PartitionSpec as P

MESH = pl.DeviceIdType.MESH
F32, BF16 = jnp.float32, jnp.bfloat16
AXIS = 4
CHIPS = 64
CHUNK = 256
MROWS = 1024


def hops(off):
    return sum(min(a, AXIS - a) for a in off)


OFFSETS = sorted(
    (
        (a, b, c)
        for a in range(AXIS)
        for b in range(AXIS)
        for c in range(AXIS)
        if (a, b, c) != (0, 0, 0)
    ),
    key=lambda off: -hops(off),
)


def coords():
    row, col = lax.axis_index("row"), lax.axis_index("col")
    x, y_lo = lax.rem(row, 4), lax.div(row, 4)
    core, y_hi, z = lax.rem(col, 2), lax.rem(lax.div(col, 2), 2), lax.div(col, 4)
    return x, y_hi * 2 + y_lo, z, core


def device(x, y, z, core):
    return (lax.rem(y, 2) * 4 + x, (z * 2 + lax.div(y, 2)) * 2 + core)


def monomials(c):
    return [
        c[0] - c[2] + c[4] - c[6],
        c[1] - 3.0 * c[3] + 5.0 * c[5] - 7.0 * c[7],
        2.0 * c[2] - 8.0 * c[4] + 18.0 * c[6],
        4.0 * c[3] - 20.0 * c[5] + 56.0 * c[7],
        8.0 * c[4] - 48.0 * c[6],
        16.0 * c[5] - 112.0 * c[7],
        32.0 * c[6],
        64.0 * c[7],
    ]


def horner(x, coefs):
    acc = coefs[-1] * x + coefs[-2]
    for c in coefs[-3::-1]:
        acc = acc * x + c
    return acc


def chirp_rows(first, width, total, steps):
    shape = (8, width)
    u = lax.broadcasted_iota(jnp.int32, shape, 1) + first
    r = lax.broadcasted_iota(jnp.int32, shape, 0)
    mask = 2 * total - 1
    step = jnp.where((r & 2) == 0, steps[0], steps[1])
    off = u & mask
    k = (((off * off) & mask) * step) & mask
    k = (k - (r & 1) * (total // 2)) & mask
    p = total // 2 - jnp.minimum(k, 2 * total - k)
    a = p.astype(F32) * (math.pi / total)
    s = a * a
    poly = horner(s, [(-1.0) ** n / math.factorial(2 * n + 1) for n in range(7)])
    return a * poly * (1.0 / math.sqrt(total))


def across(seq, r, width):
    x = jnp.broadcast_to(seq[pl.ds(r, 1), : width + 128], (128, width + 128))
    return pltpu.roll(x, 0, 1, stride=1, stride_axis=0)[:, 128:].astype(BF16)


def forward_kernel(
    total,
    design_hbm,
    coef_hbm,
    steps_hbm,
    target_hbm,
    field_out,
    dtr_ref,
    dti_ref,
    vr_ref,
    vi_ref,
    vs_ref,
    wb_ref,
    target_ref,
    field_ref,
    at_ref,
    g_ref,
    coef,
    steps,
    x_ref,
    t0,
    t1,
    wcol,
    rtab,
    qh,
    seq,
    row_seq,
    partial,
    sib,
    pieces,
    landed,
    load_sem,
    sib_send,
    sib_recv,
    rs_send,
    rs_recv,
    ag_send,
    ag_recv,
):
    rows, cols = x_ref.shape
    chunks = rows // CHUNK
    x, y, z, core = coords()
    chip = (x * AXIS + y) * AXIS + z
    other = 1 - core
    sibling = device(x, y, z, other)

    def load(i):
        part = pl.ds(pl.multiple_of(i * CHUNK, CHUNK), CHUNK)
        return pltpu.make_async_copy(design_hbm.at[part], x_ref.at[part], load_sem.at[i])

    fetches = [
        pltpu.make_async_copy(src, dst, load_sem.at[chunks + 1 + n])
        for n, (src, dst) in enumerate([(steps_hbm, steps), (coef_hbm, coef)])
    ]
    for fetch in fetches:
        fetch.start()
    for i in range(chunks):
        load(i).start()
    fetch = pltpu.make_async_copy(target_hbm, target_ref, load_sem.at[chunks])
    fetch.start()

    xs = [lax.rem(x + a, AXIS) for a in range(AXIS)]
    ys = [lax.rem(y + a, AXIS) for a in range(AXIS)]
    zs = [lax.rem(z + a, AXIS) for a in range(AXIS)]
    y_row = [lax.rem(a, 2) * AXIS for a in ys]
    y_col = [lax.div(a, 2) * 2 + core for a in ys]
    peers = [
        (
            xs[a] * (AXIS * AXIS) + ys[b] * AXIS + zs[c],
            (y_row[b] + xs[a], zs[c] * AXIS + y_col[b]),
        )
        for a, b, c in OFFSETS
    ]

    barrier = pltpu.get_barrier_semaphore()
    pl.semaphore_signal(barrier, inc=1, device_id=sibling, device_id_type=MESH)

    for _, dev in peers:
        pl.semaphore_signal(barrier, inc=1, device_id=dev, device_id_type=MESH)

    for ready in fetches:
        ready.wait()
    step = [steps[0], steps[1]]
    first_row = lax.axis_index("row") * rows - (total // 2 - 64)
    first_col = lax.axis_index("col") * cols - (total // 2 - 64)
    mono = [monomials([coef[i, k] for k in range(8)]) for i in range(2)]

    seq[:, : cols + 128] = chirp_rows(-first_col - cols, cols + 128, total, step)

    @pl.loop(0, 2)
    def _(d):
        re, im = across(seq, 2 * d, cols), across(seq, 2 * d + 1, cols)
        left = pl.ds(pl.multiple_of(256 * d, 128), 128)
        right = pl.ds(pl.multiple_of(256 * d + 128, 128), 128)
        for b in range(cols // 128):
            lo = cols - 128 - b * 128
            upper = slice(b * 128, b * 128 + 128)
            lower = slice(cols + b * 128, cols + b * 128 + 128)
            wcol[upper, left] = re[:, lo : lo + 128]
            wcol[upper, right] = im[:, lo : lo + 128]
            wcol[lower, left] = -im[:, lo : lo + 128]
            wcol[lower, right] = re[:, lo : lo + 128]

    def row_table(r):
        rtab[pl.ds(pl.multiple_of(128 * r, 128), 128), :] = across(row_seq, r, rows)

    def transmit(i, t):
        v = x_ref[pl.ds(pl.multiple_of(i * CHUNK, CHUNK), CHUNK)]
        t[:, :cols] = horner(v, mono[0]).astype(BF16)
        t[:, cols:] = horner(v, mono[1]).astype(BF16)

    def contract(i, t):
        part = pl.ds(pl.multiple_of(i * CHUNK, CHUNK), CHUNK)
        q = jnp.dot(t[...], wcol[...], preferred_element_type=F32)
        qh[part] = q.astype(BF16)

    load(0).wait()
    row_seq[...] = chirp_rows(first_row - 128, rows + 128, total, step)
    transmit(0, t0)
    @pl.loop(0, chunks // 2 - 1)
    def _(k):
        load(2 * k + 1).wait()
        load(2 * k + 2).wait()
        row_table(k)
        transmit(2 * k + 1, t1)
        contract(2 * k, t0)
        transmit(2 * k + 2, t0)
        contract(2 * k + 1, t1)

    load(chunks - 1).wait()
    row_table(3)
    transmit(chunks - 1, t1)
    contract(chunks - 2, t0)
    contract(chunks - 1, t1)

    pl.semaphore_wait(barrier, CHIPS)
    give = pltpu.make_async_remote_copy(
        src_ref=partial.at[0],
        dst_ref=sib,
        send_sem=sib_send.at[0],
        recv_sem=sib_recv.at[0],
        device_id=sibling,
        device_id_type=MESH,
    )

    @pl.loop(0, 2)
    def _(i):
        d = other + i * (2 * core - 1)
        a = rtab[pl.ds(pl.multiple_of(d * 256, 256), 256), :]
        lanes = pl.ds(pl.multiple_of(d * 256, 256), 256)
        f = jnp.dot(a, qh[:, lanes], preferred_element_type=F32)
        partial[i, :128] = f[:128, :128] - f[128:, 128:]
        partial[i, 128:] = f[:128, 128:] + f[128:, :128]

        @pl.when(i == 0)
        def _():
            give.start()

    fetch.wait()
    give.wait_recv()
    total_chip = partial[1] + sib[...]
    for p in range(CHIPS):
        pieces[p] = total_chip[4 * p : 4 * p + 4, :]

    for n, (there, dev) in enumerate(peers):
        pltpu.make_async_remote_copy(
            src_ref=pieces.at[there],
            dst_ref=landed.at[n],
            send_sem=rs_send,
            recv_sem=rs_recv,
            device_id=dev,
            device_id_type=MESH,
        ).start()

    slopes = [[k * m[k] for k in range(1, 8)] for m in mono]

    def slope(i):
        part = pl.ds(pl.multiple_of(i * 32, 32), 32)
        v = x_ref[part]
        dtr_ref[part] = horner(v, slopes[0])
        dti_ref[part] = horner(v, slopes[1])

    first = rows // 32 * 5 // 8
    pl.loop(0, first)(slope)

    everything = pl.ds(0, CHIPS - 1)
    pltpu.make_async_copy(landed.at[everything], landed.at[everything], rs_recv).wait()
    sums = [pieces[chip]] + [landed[n] for n in range(CHIPS - 1)]
    while len(sums) > 1:
        sums = [sums[n] + sums[n + 1] for n in range(0, len(sums), 2)]
    total_piece = sums[0]
    mine = field_ref.at[core]
    mine[chip] = total_piece

    for _, dev in peers:
        pltpu.make_async_remote_copy(
            src_ref=mine.at[chip],
            dst_ref=mine.at[chip],
            send_sem=ag_send,
            recv_sem=ag_recv,
            device_id=dev,
            device_id_type=MESH,
        ).start()

    pl.loop(first, rows // 32)(slope)
    seq[...] = chirp_rows(-first_row - rows, rows + 128, total, step)

    @pl.loop(0, 4)
    def _(r):
        wide = across(seq, r, rows)
        lanes = pl.ds(pl.multiple_of(128 * r, 128), 128)
        for b in range(rows // 128):
            lo = rows - 128 - b * 128
            at_ref[b * 128 : b * 128 + 128, lanes] = wide[:, lo : lo + 128]

    seq[:, : cols + 128] = chirp_rows(first_col - 128, cols + 128, total, step)

    @pl.loop(0, 2)
    def _(d):
        re, im = across(seq, 2 * d, cols), across(seq, 2 * d + 1, cols)
        part = pl.ds(pl.multiple_of(128 * d, 128), 128)
        re32, im32 = re.astype(F32), im.astype(F32)
        wb_ref[0, part] = re
        wb_ref[1, part] = (im32 - re32).astype(BF16)
        wb_ref[2, part] = (im32 + re32).astype(BF16)

    pltpu.make_async_copy(mine.at[everything], mine.at[everything], ag_recv).wait()
    show = pltpu.make_async_remote_copy(
        src_ref=mine,
        dst_ref=field_ref.at[core],
        send_sem=sib_send.at[1],
        recv_sem=sib_recv.at[1],
        device_id=sibling,
        device_id_type=MESH,
    )
    show.start()

    factor = math.sqrt(total * total) / (4.0 * 128)

    @pl.loop(0, 2)
    def _(i):
        d = core + i * (1 - 2 * core)

        @pl.when(i == 1)
        def _():
            show.wait_recv()

        for p in range(CHIPS):
            lo = 4 * p
            field_out[d, lo // 128, lo % 128 : lo % 128 + 4, :] = field_ref[d, p]
        fr, fi = field_out[d, 0], field_out[d, 1]
        excess = 4.0 * factor * (fr * fr + fi * fi - target_ref[d])
        gr, gi = excess * fr, excess * fi
        g_ref[...] = jnp.concatenate(
            [jnp.concatenate([gr, -gi], axis=1), jnp.concatenate([gi, gr], axis=1)], axis=0
        ).astype(BF16)
        near = pl.ds(pl.multiple_of(256 * d, 256), 256)
        lanes = pl.ds(pl.multiple_of(128 * d, 128), 128)

        @pl.loop(0, rows // MROWS)
        def _(j):
            part = pl.ds(pl.multiple_of(j * MROWS, MROWS), MROWS)
            v = jnp.dot(at_ref[part, near], g_ref[...], preferred_element_type=F32).astype(BF16)
            vr_ref[part, lanes] = v[:, :128]
            vi_ref[part, lanes] = v[:, 128:]
            vs_ref[part, lanes] = (v[:, :128].astype(F32) + v[:, 128:].astype(F32)).astype(BF16)

    give.wait_send()
    pltpu.make_async_copy(landed.at[everything], landed.at[everything], rs_send).wait()
    pltpu.make_async_copy(landed.at[everything], landed.at[everything], ag_send).wait()
    show.wait_send()


def backward_kernel(
    field, vr_ref, vi_ref, vs_ref, wb, dtr, dti, grad_hbm, field_hbm, out, sem, field_sem
):
    rows, cols = dtr.shape
    blocks = rows // MROWS
    show = pltpu.make_async_copy(field, field_hbm, field_sem)
    show.start()

    def write(i, n):
        slot = lax.rem(i, 2)
        lanes = pl.ds(n * 256, 256)
        return pltpu.make_async_copy(
            out.at[slot, :, lanes],
            grad_hbm.at[pl.ds(pl.multiple_of(i * MROWS, MROWS), MROWS), lanes],
            sem.at[slot, n],
        )

    @pl.loop(0, blocks)
    def _(i):
        @pl.when(i >= 2)
        def _():
            for n in range(cols // 256):
                write(i - 2, n).wait()

        part = pl.ds(pl.multiple_of(i * MROWS, MROWS), MROWS)
        slot = lax.rem(i, 2)
        for n in range(cols // 256):
            lanes = slice(n * 256, (n + 1) * 256)
            k1 = jnp.dot(vs_ref[part, :], wb[0, :, lanes], preferred_element_type=F32)
            k2 = jnp.dot(vr_ref[part, :], wb[1, :, lanes], preferred_element_type=F32)
            k3 = jnp.dot(vi_ref[part, :], wb[2, :, lanes], preferred_element_type=F32)
            out[slot, :, lanes] = dtr[part, lanes] * (k1 - k3) - dti[part, lanes] * (k1 + k2)
            write(i, n).start()

    for i in range(blocks - 2, blocks):
        for n in range(cols // 256):
            write(i, n).wait()
    show.wait()


def body(design, coefficients, focal_steps, target):
    rows, cols = design.shape
    total = rows * lax.axis_size("row")
    focal = target.shape[1]
    vmem = pl.BlockSpec(memory_space=pltpu.VMEM)
    dma = pltpu.SemaphoreType.DMA
    half = pltpu.VMEM((rows, 256), BF16)
    field, dtr, dti, vr, vi, vs, wb = pl.pallas_call(
        functools.partial(forward_kernel, total),
        out_shape=(
            pltpu.VMEM((2, 2, focal, focal), F32),
            pltpu.VMEM((rows, cols), F32),
            pltpu.VMEM((rows, cols), F32),
            half,
            half,
            half,
            pltpu.VMEM((3, 256, cols), BF16),
        ),
        in_specs=[pl.BlockSpec(memory_space=pltpu.HBM)] * 4,
        out_specs=(vmem,) * 7,
        scratch_shapes=[
            pltpu.VMEM(target.shape, F32),
            pltpu.VMEM((2, CHIPS, 4, 128), F32),
            pltpu.VMEM((rows, 512), BF16),
            pltpu.VMEM((256, 256), BF16),
            pltpu.SMEM(coefficients.shape, F32),
            pltpu.SMEM(focal_steps.shape, jnp.int32),
            pltpu.VMEM((rows, cols), F32),
            pltpu.VMEM((CHUNK, 2 * cols), BF16),
            pltpu.VMEM((CHUNK, 2 * cols), BF16),
            pltpu.VMEM((2 * cols, 512), BF16),
            pltpu.VMEM((512, rows), BF16),
            pltpu.VMEM((rows, 512), BF16),
            pltpu.VMEM((8, rows + 128), F32),
            pltpu.VMEM((8, rows + 128), F32),
            pltpu.VMEM((2, 256, 128), F32),
            pltpu.VMEM((256, 128), F32),
            pltpu.VMEM((CHIPS, 4, 128), F32),
            pltpu.VMEM((CHIPS, 4, 128), F32),
            dma((rows // CHUNK + 3,)),
            dma((2,)),
            dma((2,)),
            dma,
            dma,
            dma,
            dma,
        ],
        compiler_params=pltpu.CompilerParams(
            collective_id=0, has_side_effects=True, vmem_limit_bytes=30 * 2**20
        ),
        name="forward",
    )(*(pltpu.with_memory_space_constraint(a, pltpu.HBM) for a in (design, coefficients, focal_steps, target)))

    anywhere = pl.BlockSpec(memory_space=pl.ANY)
    gradient, field = pl.pallas_call(
        backward_kernel,
        out_shape=(
            jax.ShapeDtypeStruct((rows, cols), F32),
            jax.ShapeDtypeStruct((2, 2, focal, focal), F32),
        ),
        in_specs=[vmem] * 7,
        out_specs=(anywhere, anywhere),
        scratch_shapes=[
            pltpu.VMEM((2, MROWS, cols), F32),
            dma((2, cols // 256)),
            dma,
        ],
        compiler_params=pltpu.CompilerParams(vmem_limit_bytes=16 * 2**20),
        name="backward",
    )(field, vr, vi, vs, wb, dtr, dti)
    return gradient, field


def solution(mesh):
    return jax.shard_map(
        body,
        mesh=mesh,
        in_specs=(P("row", "col"), P(), P(), P()),
        out_specs=(P("row", "col"), P()),
        check_vma=False,
    )
```

```python
import functools
import math

import jax
import jax.numpy as jnp
from jax import lax
from jax.experimental import pallas as pl
from jax.experimental.pallas import tpu as pltpu
from jax.sharding import PartitionSpec as P

MESH = pl.DeviceIdType.MESH
F32, BF16 = jnp.float32, jnp.bfloat16
AXIS = 4
CHIPS = 64
CHUNK = 256
MROWS = 1024


def hops(off):
    return sum(min(a, AXIS - a) for a in off)


OFFSETS = sorted(
    (
        (a, b, c)
        for a in range(AXIS)
        for b in range(AXIS)
        for c in range(AXIS)
        if (a, b, c) != (0, 0, 0)
    ),
    key=lambda off: (-hops(off), off[::-1]),
)


def coords():
    row, col = lax.axis_index("row"), lax.axis_index("col")
    x, y_lo = lax.rem(row, 4), lax.div(row, 4)
    core, y_hi, z = lax.rem(col, 2), lax.rem(lax.div(col, 2), 2), lax.div(col, 4)
    return x, y_hi * 2 + y_lo, z, core


def device(x, y, z, core):
    return (lax.rem(y, 2) * 4 + x, (z * 2 + lax.div(y, 2)) * 2 + core)


def monomials(c):
    return [
        c[0] - c[2] + c[4] - c[6],
        c[1] - 3.0 * c[3] + 5.0 * c[5] - 7.0 * c[7],
        2.0 * c[2] - 8.0 * c[4] + 18.0 * c[6],
        4.0 * c[3] - 20.0 * c[5] + 56.0 * c[7],
        8.0 * c[4] - 48.0 * c[6],
        16.0 * c[5] - 112.0 * c[7],
        32.0 * c[6],
        64.0 * c[7],
    ]


def horner(x, coefs):
    acc = coefs[-1] * x + coefs[-2]
    for c in coefs[-3::-1]:
        acc = acc * x + c
    return acc


def chirp_rows(first, width, total, steps):
    shape = (8, width)
    u = lax.broadcasted_iota(jnp.int32, shape, 1) + first
    r = lax.broadcasted_iota(jnp.int32, shape, 0)
    mask = 2 * total - 1
    step = jnp.where((r & 2) == 0, steps[0], steps[1])
    off = u & mask
    k = (((off * off) & mask) * step) & mask
    k = (k - (r & 1) * (total // 2)) & mask
    p = total // 2 - jnp.minimum(k, 2 * total - k)
    a = p.astype(F32) * (math.pi / total)
    s = a * a
    poly = horner(s, [(-1.0) ** n / math.factorial(2 * n + 1) for n in range(7)])
    return a * poly * (1.0 / math.sqrt(total))


def across(seq, r, width):
    x = jnp.broadcast_to(seq[pl.ds(r, 1), : width + 128], (128, width + 128))
    return pltpu.roll(x, 0, 1, stride=1, stride_axis=0)[:, 128:].astype(BF16)


def forward_kernel(
    total,
    design_hbm,
    coef_hbm,
    steps_hbm,
    target_hbm,
    field_out,
    dtr_ref,
    dti_ref,
    vr_ref,
    vi_ref,
    vs_ref,
    wb_ref,
    target_ref,
    field_ref,
    at_ref,
    g_ref,
    coef,
    steps,
    x_ref,
    t0,
    t1,
    wcol,
    rtab,
    qh,
    seq,
    row_seq,
    partial,
    sib,
    pieces,
    landed,
    load_sem,
    sib_send,
    sib_recv,
    rs_send,
    rs_recv,
    ag_send,
    ag_recv,
):
    rows, cols = x_ref.shape
    chunks = rows // CHUNK
    x, y, z, core = coords()
    chip = (x * AXIS + y) * AXIS + z
    other = 1 - core
    sibling = device(x, y, z, other)

    def load(i):
        part = pl.ds(pl.multiple_of(i * CHUNK, CHUNK), CHUNK)
        return pltpu.make_async_copy(design_hbm.at[part], x_ref.at[part], load_sem.at[i])

    fetches = [
        pltpu.make_async_copy(src, dst, load_sem.at[chunks + 1 + n])
        for n, (src, dst) in enumerate([(steps_hbm, steps), (coef_hbm, coef)])
    ]
    for fetch in fetches:
        fetch.start()
    for i in range(chunks):
        load(i).start()
    fetch = pltpu.make_async_copy(target_hbm, target_ref, load_sem.at[chunks])
    fetch.start()

    xs = [lax.rem(x + a, AXIS) for a in range(AXIS)]
    ys = [lax.rem(y + a, AXIS) for a in range(AXIS)]
    zs = [lax.rem(z + a, AXIS) for a in range(AXIS)]
    y_row = [lax.rem(a, 2) * AXIS for a in ys]
    y_col = [lax.div(a, 2) * 2 + core for a in ys]
    peers = [
        (
            xs[a] * (AXIS * AXIS) + ys[b] * AXIS + zs[c],
            (y_row[b] + xs[a], zs[c] * AXIS + y_col[b]),
        )
        for a, b, c in OFFSETS
    ]

    barrier = pltpu.get_barrier_semaphore()
    pl.semaphore_signal(barrier, inc=1, device_id=sibling, device_id_type=MESH)

    for _, dev in peers:
        pl.semaphore_signal(barrier, inc=1, device_id=dev, device_id_type=MESH)

    for ready in fetches:
        ready.wait()
    step = [steps[0], steps[1]]
    first_row = lax.axis_index("row") * rows - (total // 2 - 64)
    first_col = lax.axis_index("col") * cols - (total // 2 - 64)
    mono = [monomials([coef[i, k] for k in range(8)]) for i in range(2)]

    seq[:, : cols + 128] = chirp_rows(-first_col - cols, cols + 128, total, step)

    @pl.loop(0, 2)
    def _(d):
        re, im = across(seq, 2 * d, cols), across(seq, 2 * d + 1, cols)
        left = pl.ds(pl.multiple_of(256 * d, 128), 128)
        right = pl.ds(pl.multiple_of(256 * d + 128, 128), 128)
        for b in range(cols // 128):
            lo = cols - 128 - b * 128
            upper = slice(b * 128, b * 128 + 128)
            lower = slice(cols + b * 128, cols + b * 128 + 128)
            wcol[upper, left] = re[:, lo : lo + 128]
            wcol[upper, right] = im[:, lo : lo + 128]
            wcol[lower, left] = -im[:, lo : lo + 128]
            wcol[lower, right] = re[:, lo : lo + 128]

    def row_table(r):
        rtab[pl.ds(pl.multiple_of(128 * r, 128), 128), :] = across(row_seq, r, rows)

    def transmit(i, t):
        v = x_ref[pl.ds(pl.multiple_of(i * CHUNK, CHUNK), CHUNK)]
        t[:, :cols] = horner(v, mono[0]).astype(BF16)
        t[:, cols:] = horner(v, mono[1]).astype(BF16)

    def contract(i, t):
        part = pl.ds(pl.multiple_of(i * CHUNK, CHUNK), CHUNK)
        q = jnp.dot(t[...], wcol[...], preferred_element_type=F32)
        qh[part] = q.astype(BF16)

    load(0).wait()
    row_seq[...] = chirp_rows(first_row - 128, rows + 128, total, step)
    transmit(0, t0)
    @pl.loop(0, chunks // 2 - 1)
    def _(k):
        load(2 * k + 1).wait()
        load(2 * k + 2).wait()
        row_table(k)
        transmit(2 * k + 1, t1)
        contract(2 * k, t0)
        transmit(2 * k + 2, t0)
        contract(2 * k + 1, t1)

    load(chunks - 1).wait()
    row_table(3)
    transmit(chunks - 1, t1)
    contract(chunks - 2, t0)
    contract(chunks - 1, t1)

    pl.semaphore_wait(barrier, CHIPS)
    give = pltpu.make_async_remote_copy(
        src_ref=partial.at[0],
        dst_ref=sib,
        send_sem=sib_send.at[0],
        recv_sem=sib_recv.at[0],
        device_id=sibling,
        device_id_type=MESH,
    )

    @pl.loop(0, 2)
    def _(i):
        d = other + i * (2 * core - 1)
        a = rtab[pl.ds(pl.multiple_of(d * 256, 256), 256), :]
        lanes = pl.ds(pl.multiple_of(d * 256, 256), 256)
        f = jnp.dot(a, qh[:, lanes], preferred_element_type=F32)
        partial[i, :128] = f[:128, :128] - f[128:, 128:]
        partial[i, 128:] = f[:128, 128:] + f[128:, :128]

        @pl.when(i == 0)
        def _():
            give.start()

    fetch.wait()
    give.wait_recv()
    total_chip = partial[1] + sib[...]
    for p in range(CHIPS):
        pieces[p] = total_chip[4 * p : 4 * p + 4, :]

    for n, (there, dev) in enumerate(peers):
        pltpu.make_async_remote_copy(
            src_ref=pieces.at[there],
            dst_ref=landed.at[n],
            send_sem=rs_send,
            recv_sem=rs_recv,
            device_id=dev,
            device_id_type=MESH,
        ).start()

    slopes = [[k * m[k] for k in range(1, 8)] for m in mono]

    def slope(i):
        part = pl.ds(pl.multiple_of(i * 32, 32), 32)
        v = x_ref[part]
        dtr_ref[part] = horner(v, slopes[0])
        dti_ref[part] = horner(v, slopes[1])

    first = rows // 32 * 5 // 8
    pl.loop(0, first)(slope)

    everything = pl.ds(0, CHIPS - 1)
    pltpu.make_async_copy(landed.at[everything], landed.at[everything], rs_recv).wait()
    sums = [pieces[chip]] + [landed[n] for n in range(CHIPS - 1)]
    while len(sums) > 1:
        sums = [sums[n] + sums[n + 1] for n in range(0, len(sums), 2)]
    total_piece = sums[0]
    mine = field_ref.at[core]
    mine[chip] = total_piece

    for _, dev in peers:
        pltpu.make_async_remote_copy(
            src_ref=mine.at[chip],
            dst_ref=mine.at[chip],
            send_sem=ag_send,
            recv_sem=ag_recv,
            device_id=dev,
            device_id_type=MESH,
        ).start()

    pl.loop(first, rows // 32)(slope)
    seq[...] = chirp_rows(-first_row - rows, rows + 128, total, step)

    @pl.loop(0, 4)
    def _(r):
        wide = across(seq, r, rows)
        lanes = pl.ds(pl.multiple_of(128 * r, 128), 128)
        for b in range(rows // 128):
            lo = rows - 128 - b * 128
            at_ref[b * 128 : b * 128 + 128, lanes] = wide[:, lo : lo + 128]

    seq[:, : cols + 128] = chirp_rows(first_col - 128, cols + 128, total, step)

    @pl.loop(0, 2)
    def _(d):
        re, im = across(seq, 2 * d, cols), across(seq, 2 * d + 1, cols)
        part = pl.ds(pl.multiple_of(128 * d, 128), 128)
        re32, im32 = re.astype(F32), im.astype(F32)
        wb_ref[0, part] = re
        wb_ref[1, part] = (im32 - re32).astype(BF16)
        wb_ref[2, part] = (im32 + re32).astype(BF16)

    pltpu.make_async_copy(mine.at[everything], mine.at[everything], ag_recv).wait()
    show = pltpu.make_async_remote_copy(
        src_ref=mine,
        dst_ref=field_ref.at[core],
        send_sem=sib_send.at[1],
        recv_sem=sib_recv.at[1],
        device_id=sibling,
        device_id_type=MESH,
    )
    show.start()

    factor = math.sqrt(total * total) / (4.0 * 128)

    @pl.loop(0, 2)
    def _(i):
        d = core + i * (1 - 2 * core)

        @pl.when(i == 1)
        def _():
            show.wait_recv()

        for p in range(CHIPS):
            lo = 4 * p
            field_out[d, lo // 128, lo % 128 : lo % 128 + 4, :] = field_ref[d, p]
        fr, fi = field_out[d, 0], field_out[d, 1]
        excess = 4.0 * factor * (fr * fr + fi * fi - target_ref[d])
        gr, gi = excess * fr, excess * fi
        g_ref[...] = jnp.concatenate(
            [jnp.concatenate([gr, -gi], axis=1), jnp.concatenate([gi, gr], axis=1)], axis=0
        ).astype(BF16)
        near = pl.ds(pl.multiple_of(256 * d, 256), 256)
        lanes = pl.ds(pl.multiple_of(128 * d, 128), 128)

        @pl.loop(0, rows // MROWS)
        def _(j):
            part = pl.ds(pl.multiple_of(j * MROWS, MROWS), MROWS)
            v = jnp.dot(at_ref[part, near], g_ref[...], preferred_element_type=F32).astype(BF16)
            vr_ref[part, lanes] = v[:, :128]
            vi_ref[part, lanes] = v[:, 128:]
            vs_ref[part, lanes] = (v[:, :128].astype(F32) + v[:, 128:].astype(F32)).astype(BF16)

    give.wait_send()
    pltpu.make_async_copy(landed.at[everything], landed.at[everything], rs_send).wait()
    pltpu.make_async_copy(landed.at[everything], landed.at[everything], ag_send).wait()
    show.wait_send()


def backward_kernel(
    field, vr_ref, vi_ref, vs_ref, wb, dtr, dti, grad_hbm, field_hbm, out, sem, field_sem
):
    rows, cols = dtr.shape
    blocks = rows // MROWS
    show = pltpu.make_async_copy(field, field_hbm, field_sem)
    show.start()

    def write(i, n):
        slot = lax.rem(i, 2)
        lanes = pl.ds(n * 256, 256)
        return pltpu.make_async_copy(
            out.at[slot, :, lanes],
            grad_hbm.at[pl.ds(pl.multiple_of(i * MROWS, MROWS), MROWS), lanes],
            sem.at[slot, n],
        )

    @pl.loop(0, blocks)
    def _(i):
        @pl.when(i >= 2)
        def _():
            for n in range(cols // 256):
                write(i - 2, n).wait()

        part = pl.ds(pl.multiple_of(i * MROWS, MROWS), MROWS)
        slot = lax.rem(i, 2)
        for n in range(cols // 256):
            lanes = slice(n * 256, (n + 1) * 256)
            k1 = jnp.dot(vs_ref[part, :], wb[0, :, lanes], preferred_element_type=F32)
            k2 = jnp.dot(vr_ref[part, :], wb[1, :, lanes], preferred_element_type=F32)
            k3 = jnp.dot(vi_ref[part, :], wb[2, :, lanes], preferred_element_type=F32)
            out[slot, :, lanes] = dtr[part, lanes] * (k1 - k3) - dti[part, lanes] * (k1 + k2)
            write(i, n).start()

    for i in range(blocks - 2, blocks):
        for n in range(cols // 256):
            write(i, n).wait()
    show.wait()


def body(design, coefficients, focal_steps, target):
    rows, cols = design.shape
    total = rows * lax.axis_size("row")
    focal = target.shape[1]
    vmem = pl.BlockSpec(memory_space=pltpu.VMEM)
    dma = pltpu.SemaphoreType.DMA
    half = pltpu.VMEM((rows, 256), BF16)
    field, dtr, dti, vr, vi, vs, wb = pl.pallas_call(
        functools.partial(forward_kernel, total),
        out_shape=(
            pltpu.VMEM((2, 2, focal, focal), F32),
            pltpu.VMEM((rows, cols), F32),
            pltpu.VMEM((rows, cols), F32),
            half,
            half,
            half,
            pltpu.VMEM((3, 256, cols), BF16),
        ),
        in_specs=[pl.BlockSpec(memory_space=pltpu.HBM)] * 4,
        out_specs=(vmem,) * 7,
        scratch_shapes=[
            pltpu.VMEM(target.shape, F32),
            pltpu.VMEM((2, CHIPS, 4, 128), F32),
            pltpu.VMEM((rows, 512), BF16),
            pltpu.VMEM((256, 256), BF16),
            pltpu.SMEM(coefficients.shape, F32),
            pltpu.SMEM(focal_steps.shape, jnp.int32),
            pltpu.VMEM((rows, cols), F32),
            pltpu.VMEM((CHUNK, 2 * cols), BF16),
            pltpu.VMEM((CHUNK, 2 * cols), BF16),
            pltpu.VMEM((2 * cols, 512), BF16),
            pltpu.VMEM((512, rows), BF16),
            pltpu.VMEM((rows, 512), BF16),
            pltpu.VMEM((8, rows + 128), F32),
            pltpu.VMEM((8, rows + 128), F32),
            pltpu.VMEM((2, 256, 128), F32),
            pltpu.VMEM((256, 128), F32),
            pltpu.VMEM((CHIPS, 4, 128), F32),
            pltpu.VMEM((CHIPS, 4, 128), F32),
            dma((rows // CHUNK + 3,)),
            dma((2,)),
            dma((2,)),
            dma,
            dma,
            dma,
            dma,
        ],
        compiler_params=pltpu.CompilerParams(
            collective_id=0, has_side_effects=True, vmem_limit_bytes=30 * 2**20
        ),
        name="forward",
    )(*(pltpu.with_memory_space_constraint(a, pltpu.HBM) for a in (design, coefficients, focal_steps, target)))

    anywhere = pl.BlockSpec(memory_space=pl.ANY)
    gradient, field = pl.pallas_call(
        backward_kernel,
        out_shape=(
            jax.ShapeDtypeStruct((rows, cols), F32),
            jax.ShapeDtypeStruct((2, 2, focal, focal), F32),
        ),
        in_specs=[vmem] * 7,
        out_specs=(anywhere, anywhere),
        scratch_shapes=[
            pltpu.VMEM((2, MROWS, cols), F32),
            dma((2, cols // 256)),
            dma,
        ],
        compiler_params=pltpu.CompilerParams(vmem_limit_bytes=16 * 2**20),
        name="backward",
    )(field, vr, vi, vs, wb, dtr, dti)
    return gradient, field


def solution(mesh):
    return jax.shard_map(
        body,
        mesh=mesh,
        in_specs=(P("row", "col"), P(), P(), P()),
        out_specs=(P("row", "col"), P()),
        check_vma=False,
    )
```
